256 devices in a mesh: row: 16 (over x, y_lo, core), col: 16 (over y_hi, z).
Axes of the slice: x: 4, y: 4 (y_hi: 2, y_lo: 2; y = y_hi * 2 + y_lo), z: 8, core: 2. Of those that a mesh axis runs over, the one named last changes fastest.
Arguments:
- tcc_before: bfloat16 [16384, 16384], P('row', 'col'), as said below
- shift_panel: bfloat16 [16384, 512], P(('row', 'col')), may hold values from -0.046875 to 0.046875
- source_map: float32 [1024], replicated, may hold values from 0.1 to 1
- pixels: int32 [512], replicated, may hold values from 0 to 1023
- start_vectors: float32 [16384, 128], P(('row', 'col')), may hold values from -6 to 6
Outputs:
- filtered: float32 [16384, 128], P(('row', 'col'))
- tcc: bfloat16 [16384, 16384], P('row', 'col')
The draws below stay inside these ranges and needn't reach their ends.
Inputs may be any that keep to these rules, and one draw needn't show every extreme that they name: tcc_before is exactly symmetric.
All inputs are finite; a program needn't handle non-finite values.
Results may differ from the reference program's by a relative error of at most 0.022.
Values may be sent and summed in bfloat16 or wider, within the bound.
A program may use at most 64 MiB of HBM per device.

```python
import math
import jax
import jax.numpy as jnp
from jax import lax

NM = 16384
ZONE = 512
SRC = 1024
VECS = 128
DEGREES = 4


def draw_tcc_before(key, part):
    key = jax.random.fold_in(key, 11)
    base = jax.random.normal(key, (NM, NM), jnp.float32)
    return ((base + base.T) * (0.35355339 / math.sqrt(NM))).astype(jnp.bfloat16)


def set_ends(drawn, key, least, largest):
    spot = [jax.random.randint(jax.random.fold_in(key, axis), (), 0, length) for axis, length in enumerate(drawn.shape)]
    main_axis = drawn.shape.index(max(drawn.shape))
    beside = spot[:main_axis] + [(spot[main_axis] + 1) % drawn.shape[main_axis]] + spot[main_axis + 1:]
    return drawn.at[tuple(spot)].set(least).at[tuple(beside)].set(largest)


def block_scale(rng, dims, shards, low, largest):
    factor_of = 1.0
    for position, shards_of in shards:
        steps = jax.random.uniform(jax.random.fold_in(jax.random.fold_in(rng, 6), position), (shards_of,), jnp.float32, low / len(shards), largest / len(shards))
        factor_of = factor_of * jnp.repeat(jnp.exp(steps), dims[position] // shards_of).reshape((-1,) + (1,) * (len(dims) - 1 - position))
    return factor_of


def normal_values(rng, extent, scale, limit, pieces=(), kind=jnp.bfloat16):
    result = jax.random.normal(rng, extent, jnp.float32) * scale
    if len(pieces) > 0:
        result = block_scale(rng, extent, pieces, -0.22, 0.18) * result
    return jnp.clip(result, min=-limit, max=limit).astype(kind)


def setup_inputs(seed: int = 0) -> dict:
    keys = jax.random.split(jax.random.key(seed), 6)
    return {
        "tcc_before": draw_tcc_before(jax.random.fold_in(keys[5], 71), 0),
        "shift_panel": normal_values(keys[1], (NM, ZONE), NM ** -0.5, 0.046875, ((0, 256),)),
        "source_map": jnp.clip(jnp.exp(jax.random.uniform(keys[2], (SRC,), jnp.float32, math.log(0.1), math.log(1.0))), 0.1, 1.0),
        "pixels": set_ends(jax.random.randint(keys[3], (ZONE,), 0, SRC), jax.random.fold_in(keys[3], 1), 0, SRC - 1).astype(jnp.int32),
        "start_vectors": normal_values(keys[4], (NM, VECS), 1.0, 6.0, ((0, 256),), jnp.float32),
    }


CENTER = 0.45
HALF_WIDTH = 1.6

def zone_panels(shift_panel, source_map, pixels):
    hit = pixels[:, None] == jnp.arange(SRC, dtype=jnp.int32)[None, :]
    weight = lax.optimization_barrier(jnp.sum(jnp.where(hit, source_map[None, :], jnp.float32(0.0)), axis=1))
    scaled = (shift_panel.astype(jnp.float32) * jnp.sqrt(weight)[None, :]).astype(jnp.bfloat16)
    half = NM // 2
    turned = jnp.concatenate([-scaled[half:], scaled[:half]], axis=0)
    return jnp.concatenate([scaled, turned], axis=1)

def reference(tcc_before, shift_panel, source_map, pixels, start_vectors):
    both = zone_panels(shift_panel, source_map, pixels)
    block = min(NM, 2048)

    def one_block(index):
        first = (index * block).astype(jnp.int32)
        left = lax.dynamic_slice_in_dim(both, first, block, 0)
        update = lax.dot_general(left, both, (((1,), (1,)), ((), ())), preferred_element_type=jnp.float32)
        old = lax.dynamic_slice_in_dim(tcc_before, first, block, 0).astype(jnp.float32)
        return (old + update).astype(jnp.bfloat16)
    tcc = lax.map(one_block, jnp.arange(NM // block, dtype=jnp.int32)).reshape(NM, NM)
    previous = start_vectors
    current_b = previous.astype(jnp.bfloat16)
    image = jnp.dot(tcc, current_b, preferred_element_type=jnp.float32)
    current = (image - CENTER * current_b.astype(jnp.float32)) / HALF_WIDTH
    for degree in range(1, DEGREES):
        current_b = current.astype(jnp.bfloat16)
        image = jnp.dot(tcc, current_b, preferred_element_type=jnp.float32)
        following = 2.0 / HALF_WIDTH * (image - CENTER * current_b.astype(jnp.float32)) - previous
        previous, current = (current, following)
    return (current, tcc)
```

```python
import jax
import jax.numpy as jnp
from jax import lax
from jax.experimental import pallas as pl
from jax.experimental.pallas import tpu as pltpu
from jax.sharding import PartitionSpec as P

DEGREES = 4
CENTER = 0.45
HALF_WIDTH = 1.6
MESH = pl.DeviceIdType.MESH
N = 16
ROWS = 64
f32 = jnp.float32
bf16 = jnp.bfloat16


def mod(value, size):
    return lax.rem(value + size, size)


def device(x, y, core, z):
    x, y, z = mod(x, 4), mod(y, 4), mod(z, 8)
    return (4 * x + 2 * lax.rem(y, 2) + core, 8 * (y // 2) + z)


def body(
    before, panel, source, pixels, start, filtered, tcc,
    left, right, tile, gathered, partial, arrived, outgoing,
    tcc_sem, quad_send, quad_recv, ring_send, ring_recv, turn_send, turn_recv,
    block_send, block_recv, gather_send, gather_recv, sum_send, sum_recv,
):
    row, col = lax.axis_index("row"), lax.axis_index("col")
    x, y_lo, core = row // 4, lax.rem(row // 2, 2), lax.rem(row, 2)
    y_hi, z = col // 8, lax.rem(col, 8)
    y = 2 * y_hi + y_lo
    half = x // 2
    kind = lax.rem(row, 8)
    a, b, k = z // 4, lax.rem(z // 2, 2), lax.rem(z, 2)

    load = pltpu.make_async_copy(before, tile, tcc_sem.at[0])
    load.start()

    def peer(axis, index):
        return (index, col) if axis == "row" else (row, index)

    barrier = pltpu.get_barrier_semaphore()

    @pl.loop(1, N)
    def _(step):
        pl.semaphore_signal(barrier, 1, device_id=peer("row", mod(row + step, N)), device_id_type=MESH)
        pl.semaphore_signal(barrier, 1, device_id=peer("col", mod(col + step, N)), device_id_type=MESH)

    far = jnp.where(y_lo == 0, y - 1, y + 1)
    pl.semaphore_signal(barrier, 1, device_id=device(x, far + 4, core, z), device_id_type=MESH)
    pl.semaphore_signal(barrier, 1, device_id=device(x + 2, y + 2, core, z), device_id_type=MESH)

    src = jnp.broadcast_to(source[...], (N, source.shape[1]))
    high = src.astype(bf16).astype(f32)
    middle = (src - high).astype(bf16).astype(f32)
    low = src - high - middle
    part = lax.broadcasted_iota(jnp.int32, src.shape, 0)
    parts = jnp.where(part == 0, high, jnp.where(part == 1, middle, jnp.where(part == 2, low, 0.0)))
    place = lax.broadcasted_iota(jnp.int32, (source.shape[1], pixels.shape[1]), 0)
    hit = jnp.where(place == pixels[...], 1.0, 0.0).astype(bf16)
    three = jnp.dot(parts.astype(bf16), hit, preferred_element_type=f32)
    weight = three[0:1] + three[1:2] + three[2:3]
    scaled = (panel[...].astype(f32) * jnp.sqrt(weight)).astype(bf16)
    left[half, y_hi, z] = scaled
    outgoing[0] = start[...].astype(bf16)

    @pl.when(kind == z)
    def _():
        right[half, y_hi, z] = scaled

    pl.semaphore_wait(barrier, 2 * (N - 1) + 2)

    def remote(src_ref, dst_ref, send, recv, to):
        return pltpu.make_async_remote_copy(
            src_ref=src_ref, dst_ref=dst_ref, send_sem=send, recv_sem=recv, device_id=to, device_id_type=MESH
        )

    own = left.at[half, y_hi, z]

    def quad_place(q):
        return mod(half + q % 2, 2), mod(y_hi + q // 2, 2)

    def quad(q):
        return remote(own, own, quad_send.at[q], quad_recv.at[q], device(x + 2 * (q % 2), y + 2 * (q // 2), core, z))

    def quad_wait(q):
        there = left.at[quad_place(q)[0], quad_place(q)[1], z]
        remote(there, there, quad_send.at[q], quad_recv.at[q], (row, col)).wait_recv()

    for q in (1, 2, 3):
        quad(q).start()

    def turn():
        return remote(own, right.at[half, y_hi, z], turn_send.at[0], turn_recv.at[z], device(x, y, core, kind))

    @pl.when(kind != z)
    def _():
        turn().start()

    def ring(way, step, q):
        h, yh = quad_place(q)
        at = left.at[h, yh, mod(z - step if way == 0 else z + step, 8) if step else z]
        return remote(
            at, at, ring_send.at[way, step, q], ring_recv.at[way, step, q],
            device(x, y, core, z + 1 if way == 0 else z + 7),
        )

    def ring_wait(way, step, q):
        h, yh = quad_place(q)
        at = left.at[h, yh, mod(z - step - 1 if way == 0 else z + step + 1, 8)]
        remote(at, at, ring_send.at[way, step, q], ring_recv.at[way, step, q], (row, col)).wait_recv()

    def ring_step(step):
        for q in range(4):
            if step == 0 and q > 0:
                quad_wait(q)
            for way in (0, 1):
                if step > 0:
                    ring_wait(way, step - 1, q)
                if step < 3 or (q < 2) == (way == 0):
                    ring(way, step, q).start()

    x_match, y_match, holder = lax.rem(x, 2) == a, y_lo == b, core == k
    near = jnp.where(x_match, half, mod(x + 3, 4) // 2)
    down, up = mod(y + 3, 4) // 2, mod(y + 1, 4) // 2

    def turns(i):
        mine = (near if i < 2 else 1 - near, i % 2)
        other = ((near, 1 - near, near, 1 - near)[i], (0, 1, 1, 0)[i])
        return jnp.where(x_match, mine[0], other[0]), jnp.where(x_match, mine[1], other[1])

    def block(h, yh, p):
        return right.at[h, yh, pl.ds(4 * p, 4)]

    def block_copy(h, yh, p, way):
        to = (
            device(x + 1, y, core, z), device(x + 3, y, core, z),
            device(x, y + 1, core, z), device(x, y + 3, core, z), device(x, y, 1 - core, z),
        )[way]
        at = block(h, yh, p)
        index = 4 * h + 2 * yh + p
        return remote(at, at, block_send.at[index, way], block_recv.at[index], to)

    def block_wait(h, yh, p):
        at = block(h, yh, p)
        remote(at, at, block_send.at[0, 0], block_recv.at[4 * h + 2 * yh + p], (row, col)).wait_recv()

    def flow(op):
        starting = op == "start"

        def go(*which):
            copy = block_copy(*which)
            copy.start() if starting else copy.wait_send()

        def arrive(*which):
            if starting:
                block_wait(*which)

        def first():
            @pl.when(x_match & y_match & holder)
            def _():
                if starting:
                    @pl.loop(1, 8)
                    def _(step):
                        other = mod(z + step, 8)
                        at = right.at[half, y_hi, other]
                        remote(at, at, turn_send.at[0], turn_recv.at[other], (row, col)).wait_recv()
                for p, way in ((0, 0), (1, 1), (1, 0), (0, 1)):
                    go(half, y_hi, p, way)
                for p in (0, 1):
                    for way in (2, 3, 4):
                        go(half, y_hi, p, way)

        def second():
            @pl.when(jnp.logical_not(x_match) & y_match & holder)
            def _():
                for i in range(2):
                    h, p = turns(i)
                    arrive(h, y_hi, p)
                    go(h, y_hi, p, i)
                    for way in (2, 3, 4):
                        go(h, y_hi, p, way)

        def third():
            @pl.when(y_match & holder)
            def _():
                for i in range(2, 4):
                    h, p = turns(i)
                    arrive(h, y_hi, p)
                    for way in (2, 3, 4):
                        go(h, y_hi, p, way)

        def fourth():
            @pl.when(jnp.logical_not(y_match) & holder)
            def _():
                for i in range(4):
                    h, p = turns(i)
                    for yh, way in ((down, 2), (up, 3)):
                        arrive(h, yh, p)
                        passing = h == (0 if way == 2 else 1)

                        @pl.when(passing)
                        def _():
                            go(h, yh, p, way)

                        go(h, yh, p, 4)

        def fifth():
            @pl.when(y_match & holder)
            def _():
                for i in range(4):
                    h, p = turns(i)
                    arrive(h, 1 - y_hi, p)
                    go(h, 1 - y_hi, p, 4)

        return first, second, third, fourth, fifth

    first, second, third, fourth, fifth = flow("start")
    ring_step(0)
    first()
    ring_step(1)
    second()
    ring_step(2)
    third()
    ring_step(3)

    def gather_start(stage, axis):
        me = row if axis == "row" else col
        piece = pl.ds(pl.multiple_of(me * ROWS, ROWS), ROWS)
        gathered[stage, piece] = outgoing[stage]

        @pl.loop(1, N)
        def _(step):
            to = mod(me + step, N)
            remote(
                outgoing.at[stage], gathered.at[stage, piece], gather_send.at[stage, to], gather_recv.at[stage, me],
                peer(axis, to),
            ).start()

    def gather_wait(stage, axis):
        me = row if axis == "row" else col

        @pl.loop(1, N)
        def _(step):
            other = mod(me + step, N)
            at = gathered.at[stage, pl.ds(pl.multiple_of(other * ROWS, ROWS), ROWS)]
            remote(at, at, gather_send.at[stage, other], gather_recv.at[stage, other], (row, col)).wait_recv()

    def sum_send_piece(stage, axis, to):
        me = row if axis == "row" else col
        return remote(
            partial.at[stage, pl.ds(pl.multiple_of(to * ROWS, ROWS), ROWS)], arrived.at[stage, me],
            sum_send.at[stage, to], sum_recv.at[stage, me], peer(axis, to),
        )

    def sum_wait(stage, axis, total):
        me = row if axis == "row" else col

        def add(step, total):
            other = mod(me + step, N)
            at = arrived.at[stage, other]
            remote(at, at, sum_send.at[stage, other], sum_recv.at[stage, other], (row, col)).wait_recv()
            return total + at[...].astype(f32)

        return lax.fori_loop(1, N, add, total)

    gather_start(0, "col")
    fourth()
    fifth()
    for q in range(4):
        for way in (0, 1):
            if (q < 2) == (way == 0):
                ring_wait(way, 3, q)

    @pl.when(jnp.logical_not(holder))
    def _():
        for h in range(2):
            for yh in range(2):
                for p in range(2):
                    block_wait(h, yh, p)

    load.wait()
    sign = jnp.where(half == y_hi, 1.0, -1.0).astype(f32)
    nt = (((1,), (1,)), ((), ()))

    @pl.loop(0, 8)
    def _(i):
        yh, zs = i // 4, pl.ds(2 * lax.rem(i, 4), 2)
        span = pl.ds(pl.multiple_of(i * 128, 128), 128)
        straight = lax.dot_general(
            left[half, yh, zs].reshape(128, 512), right[y_hi].reshape(1024, 512), nt, preferred_element_type=f32
        )
        turned = lax.dot_general(
            left[1 - half, yh, zs].reshape(128, 512), right[1 - y_hi].reshape(1024, 512), nt,
            preferred_element_type=f32,
        )
        tile[span] = (tile[span].astype(f32) + (straight + sign * turned)).astype(bf16)

    store = pltpu.make_async_copy(tile, tcc, tcc_sem.at[1])
    store.start()

    centre = jnp.where(row == col, CENTER, 0.0).astype(f32)
    mine = []
    for stage in range(DEGREES):
        axis, over = ("col", "row") if stage % 2 == 0 else ("row", "col")
        me = row if over == "row" else col
        if stage > 0:
            gather_start(stage, axis)
        gather_wait(stage, axis)
        vectors = gathered.at[stage]
        if stage % 2 == 0:
            turned_vectors = vectors[...].T
        for i in range(4):
            span = pl.ds(256 * i, 256)
            if stage % 2 == 0:
                image = jnp.dot(turned_vectors, tile[:, span], preferred_element_type=f32).T
            else:
                image = jnp.dot(tile[span], vectors[...], preferred_element_type=f32)
            image = image - centre * vectors[span].astype(f32)
            partial[stage, span] = image.astype(bf16)
            for j in range(4):
                to = 4 * i + j

                @pl.when(me == to)
                def _():
                    filtered[...] = image[ROWS * j:ROWS * (j + 1)]

                @pl.when(me != to)
                def _():
                    sum_send_piece(stage, over, to).start()
        total = sum_wait(stage, over, filtered[...])
        if stage == 0:
            current = total / HALF_WIDTH
        else:
            current = 2.0 / HALF_WIDTH * total - (mine[stage - 2] if stage > 1 else start[...])
        mine.append(current)
        if stage < DEGREES - 1:
            outgoing[stage + 1] = current.astype(bf16)
    filtered[...] = mine[-1]

    store.wait()
    for q in (1, 2, 3):
        quad(q).wait_send()

    @pl.when(kind != z)
    def _():
        turn().wait_send()

    for step in range(4):
        for q in range(4):
            for way in (0, 1):
                if step < 3 or (q < 2) == (way == 0):
                    ring(way, step, q).wait_send()
    for part_of in flow("wait"):
        part_of()
    for stage in range(DEGREES):
        axis, over = ("col", "row") if stage % 2 == 0 else ("row", "col")

        @pl.loop(1, N)
        def _(step):
            to = mod((row if axis == "row" else col) + step, N)
            at = outgoing.at[stage]
            remote(at, at, gather_send.at[stage, to], gather_recv.at[stage, to], (row, col)).wait_send()
            to = mod((row if over == "row" else col) + step, N)
            sum_send_piece(stage, over, to).wait_send()


def on_device(tcc_before, shift_panel, source_map, pixels, start_vectors):
    vmem = pl.BlockSpec(memory_space=pltpu.VMEM)
    anywhere = pl.BlockSpec(memory_space=pl.ANY)
    dma = pltpu.SemaphoreType.DMA
    return pl.pallas_call(
        body,
        out_shape=(
            jax.ShapeDtypeStruct(start_vectors.shape, f32),
            jax.ShapeDtypeStruct(tcc_before.shape, bf16),
        ),
        in_specs=[anywhere, vmem, vmem, vmem, vmem],
        out_specs=(vmem, anywhere),
        scratch_shapes=[
            pltpu.VMEM((2, 2, 8, ROWS, 512), bf16),
            pltpu.VMEM((2, 2, 8, ROWS, 512), bf16),
            pltpu.VMEM((1024, 1024), bf16),
            pltpu.VMEM((DEGREES, 1024, 128), bf16),
            pltpu.VMEM((DEGREES, 1024, 128), bf16),
            pltpu.VMEM((DEGREES, N, ROWS, 128), bf16),
            pltpu.VMEM((DEGREES, ROWS, 128), bf16),
            dma((2,)), dma((4,)), dma((4,)), dma((2, 4, 4)), dma((2, 4, 4)), dma((1,)), dma((8,)),
            dma((8, 5)), dma((8,)), dma((DEGREES, N)), dma((DEGREES, N)), dma((DEGREES, N)), dma((DEGREES, N)),
        ],
        compiler_params=pltpu.CompilerParams(
            collective_id=0, has_side_effects=True, vmem_limit_bytes=40 * 1024 * 1024
        ),
    )(tcc_before, shift_panel, source_map.reshape(1, -1), pixels.reshape(1, -1), start_vectors)


def solution(mesh):
    in_specs = (P("row", "col"), P(("row", "col"), None), P(), P(), P(("row", "col"), None))
    out_specs = (P(("row", "col"), None), P("row", "col"))
    return jax.shard_map(
        on_device, mesh=mesh, in_specs=in_specs, out_specs=out_specs, check_vma=False
    )
```

```python
import jax
import jax.numpy as jnp
from jax import lax
from jax.experimental import pallas as pl
from jax.experimental.pallas import tpu as pltpu
from jax.sharding import PartitionSpec as P

DEGREES = 4
CENTER = 0.45
HALF_WIDTH = 1.6
MESH = pl.DeviceIdType.MESH
N = 16
ROWS = 64
ZONE = 512
WINDOW = 2


def farthest_first(moves, hops):
    return sorted(moves, key=lambda move: -hops(*move))


ALONG_Z = (4, 3, -3, 2, -2, 1, -1, 0)
COL_MOVES = farthest_first(
    [(dy, dz) for dy in (1, 0) for dz in ALONG_Z if dy or dz], lambda dy, dz: 2 * dy + abs(dz)
)
ROW_MOVES = farthest_first(
    [(dx, dy, dk) for dx in (2, 1, -1, 0) for dy in (1, 0) for dk in (1, 0) if dx or dy or dk],
    lambda dx, dy, dk: abs(dx) + dy,
)
PLANE_MOVES = [move for move in ROW_MOVES if move[2] == 0]
f32 = jnp.float32
bf16 = jnp.bfloat16


def mod(value, size):
    return lax.rem(value + size, size)


def device(x, y, core, z):
    x, y, z = mod(x, 4), mod(y, 4), mod(z, 8)
    return (4 * x + 2 * lax.rem(y, 2) + core, 8 * (y // 2) + z)


def body(
    before, panel_in, source_in, pixels_in, start_in, filtered_out, tcc,
    panel, source, pixels, start, filtered, left, right, tile, gathered, partial, arrived, outgoing,
    whole, history,
    tcc_sem, quad_send, quad_recv, ring_send, ring_recv, turn_send,
    piece_send, piece_recv, gather_send, gather_recv, pass_send, pass_recv, sum_send, sum_recv,
):
    row, col = lax.axis_index("row"), lax.axis_index("col")
    x, y_lo, core = row // 4, lax.rem(row // 2, 2), lax.rem(row, 2)
    y_hi, z = col // 8, lax.rem(col, 8)
    y = 2 * y_hi + y_lo
    half = x // 2
    kind = lax.rem(row, 8)
    here = (row, col)
    sibling = (row + 1 - 2 * core, col)

    loads = [
        pltpu.make_async_copy(src, dst, tcc_sem.at[2 + i])
        for i, (src, dst) in enumerate(
            ((pixels_in, pixels), (source_in, source), (panel_in, panel), (start_in, start))
        )
    ]
    for small in loads:
        small.start()
    load = pltpu.make_async_copy(before, tile, tcc_sem.at[0])
    load.start()

    barrier = pltpu.get_barrier_semaphore()

    @pl.loop(1, N)
    def _(step):
        pl.semaphore_signal(barrier, 1, device_id=(mod(row + step, N), col), device_id_type=MESH)
        pl.semaphore_signal(barrier, 1, device_id=(row, mod(col + step, N)), device_id_type=MESH)

    far = jnp.where(y_lo == 0, y - 1, y + 1)
    swapped = (8 * half + z, 8 * y_hi + kind)
    for to in (device(x, far + 4, core, z), device(x + 2, y + 2, core, z), swapped):
        pl.semaphore_signal(barrier, 1, device_id=to, device_id_type=MESH)

    for small in loads:
        small.wait()
    src = jnp.broadcast_to(source[...], (N, source.shape[1]))
    high = src.astype(bf16).astype(f32)
    middle = (src - high).astype(bf16).astype(f32)
    low = src - high - middle
    part = lax.broadcasted_iota(jnp.int32, src.shape, 0)
    parts = jnp.where(part == 0, high, jnp.where(part == 1, middle, jnp.where(part == 2, low, 0.0)))
    place = lax.broadcasted_iota(jnp.int32, (source.shape[1], pixels.shape[1]), 0)
    hit = jnp.where(place == pixels[...], 1.0, 0.0).astype(bf16)
    three = jnp.dot(parts.astype(bf16), hit, preferred_element_type=f32)
    weight = three[0:1] + three[1:2] + three[2:3]
    scaled = (panel[...].astype(f32) * jnp.sqrt(weight)).astype(bf16)
    left[half, y_hi, z, :, :ZONE] = scaled
    left[half, y_hi, z, :, ZONE:] = start[...].astype(bf16)

    @pl.when(kind == z)
    def _():
        right[half, y_hi, z] = scaled

    pl.semaphore_wait(barrier, 2 * (N - 1) + 3)

    def remote(src_ref, dst_ref, send, recv, to):
        return pltpu.make_async_remote_copy(
            src_ref=src_ref, dst_ref=dst_ref, send_sem=send, recv_sem=recv, device_id=to, device_id_type=MESH
        )

    def turn():
        return remote(
            left.at[half, y_hi, z, :, pl.ds(0, ZONE)], right.at[half, y_hi, z], turn_send.at[0],
            piece_recv.at[half, y_hi, z], swapped,
        )

    @pl.when(kind != z)
    def _():
        turn().start()

    def chip(i, j):
        along_x, along_y = jnp.where(core == 0, i, j), jnp.where(core == 0, j, i)
        return mod(x + along_x, 4), mod(y + along_y, 4)

    def place_of(cx, cy, k):
        return cx // 2, cy // 2, 4 * lax.rem(cx, 2) + 2 * lax.rem(cy, 2) + k

    def piece_copy(i, j, way):
        at = place_of(*chip(i, j), core)
        if way is None:
            index, to = 6, sibling
        else:
            tx, ty = chip(*way)
            index, to = (way[0] or 3 + way[1]) - 1, device(tx, ty, core, z)
        return remote(right.at[at], right.at[at], piece_send.at[i, j, index], piece_recv.at[at], to)

    def piece_wait(i, j, k=None):
        cx, cy = chip(i, j)
        at = place_of(cx, cy, core if k is None else k)
        remote(right.at[at], right.at[at], turn_send.at[0], piece_recv.at[at], here).wait_recv()

    def piece_first():
        @pl.when(kind != z)
        def _():
            piece_wait(0, 0)

        for d in (2, 1, 3):
            piece_copy(0, 0, (d, 0)).start()
        for d in (2, 1, 3):
            piece_copy(0, 0, (0, d)).start()
        piece_copy(0, 0, None).start()

    def piece_second():
        for i in (1, 3, 2):
            piece_wait(i, 0)
            for d in (2, 1, 3):
                piece_copy(i, 0, (0, d)).start()
            piece_copy(i, 0, None).start()

    def piece_third():
        for i in (0, 1, 3, 2):
            for j in (1, 3, 2):
                piece_wait(i, j)
                piece_copy(i, j, None).start()

    def piece_last():
        for i in range(4):
            for j in range(4):
                piece_wait(i, j, 1 - core)

    def piece_sent():
        for i in range(4):
            for j in range(4):
                piece_copy(i, j, None).wait_send()
                if j == 0:
                    for d in (1, 2, 3):
                        piece_copy(i, 0, (0, d)).wait_send()
                        if i == 0:
                            piece_copy(0, 0, (d, 0)).wait_send()

    def piece_of(q, zz):
        h, yh = mod(half + q % 2, 2), mod(y_hi + q // 2, 2)
        return left.at[h, yh, zz] if q % 2 == 0 else left.at[h, yh, zz, :, pl.ds(0, ZONE)]

    def quad(q):
        own = left.at[half, y_hi, z]
        own = own if q % 2 == 0 else left.at[half, y_hi, z, :, pl.ds(0, ZONE)]
        return remote(own, own, quad_send.at[q], quad_recv.at[q], device(x + 2 * (q % 2), y + 2 * (q // 2), core, z))

    def quad_wait(q):
        there = piece_of(q, z)
        remote(there, there, quad_send.at[q], quad_recv.at[q], here).wait_recv()

    def ring(way, step, q):
        at = piece_of(q, mod(z - step if way == 0 else z + step, 8))
        return remote(
            at, at, ring_send.at[way, step, q], ring_recv.at[way, step, q],
            device(x, y, core, z + 1 if way == 0 else z + 7),
        )

    def ring_wait(way, step, q):
        at = piece_of(q, mod(z - step - 1 if way == 0 else z + step + 1, 8))
        remote(at, at, ring_send.at[way, step, q], ring_recv.at[way, step, q], here).wait_recv()

    in_flight = [[], []]

    def ring_start(way, step, q):
        if len(in_flight[way]) == WINDOW:
            ring(way, *in_flight[way].pop(0)).wait_send()
        ring(way, step, q).start()
        in_flight[way].append((step, q))

    def ring_step(step):
        for q in range(4):
            if step == 0 and q > 0:
                quad_wait(q)
            for way in (0, 1):
                if step > 0:
                    ring_wait(way, step - 1, q)
                if step < 3 or (q < 2) == (way == 0):
                    ring_start(way, step, q)

    for q in (1, 2, 3):
        quad(q).start()
    ring_step(0)
    piece_first()
    ring_step(1)
    piece_second()
    ring_step(2)
    piece_third()
    ring_step(3)
    piece_last()
    load.wait()
    for q in range(4):
        for way in (0, 1):
            if (q < 2) == (way == 0):
                ring_wait(way, 3, q)

    sign = jnp.where(half == y_hi, 1.0, -1.0).astype(f32)
    nt = (((1,), (1,)), ((), ()))

    @pl.loop(0, 4)
    def _(i):
        yh, zs = i // 2, pl.ds(4 * lax.rem(i, 2), 4)
        span = pl.ds(pl.multiple_of(i * 256, 256), 256)
        straight = lax.dot_general(
            left[half, yh, zs, :, :ZONE].reshape(256, ZONE), right[y_hi].reshape(1024, ZONE), nt,
            preferred_element_type=f32,
        )
        turned = lax.dot_general(
            left[1 - half, yh, zs, :, :ZONE].reshape(256, ZONE), right[1 - y_hi].reshape(1024, ZONE), nt,
            preferred_element_type=f32,
        )
        tile[span] = (tile[span].astype(f32) + (straight + sign * turned)).astype(bf16)

    store = pltpu.make_async_copy(tile, tcc, tcc_sem.at[1])
    store.start()

    def member(axis, move):
        if axis == "row":
            dx, dy, dk = move
            return 4 * mod(x + dx, 4) + 2 * mod(y_lo + dy, 2) + mod(core + dk, 2)
        dy, dz = move
        return 8 * mod(y_hi + dy, 2) + mod(z + dz, 8)

    def back(axis, move):
        return tuple(-d for d in move)

    def address(axis, index):
        return (index, col) if axis == "row" else (row, index)

    def rows_of(index):
        return pl.ds(pl.multiple_of(index * ROWS, ROWS), ROWS)

    most = pl.ds(0, (N - 1) * ROWS)

    def gather_col(stage):
        def copy(move):
            at = gathered.at[stage, rows_of(col)]
            return remote(
                outgoing.at[stage], at, gather_send.at[stage], gather_recv.at[stage], address("col", member("col", move))
            )

        gathered[stage, rows_of(col)] = outgoing[stage]
        for move in COL_MOVES:
            copy(move).start()

        def wait():
            every = gathered.at[stage, most]
            remote(every, every, gather_send.at[stage], gather_recv.at[stage], here).wait()

        return wait

    def gather_row(stage):
        which = stage // 2

        def copy(n, move):
            at = gathered.at[stage, rows_of(row)]
            return remote(
                outgoing.at[stage], at, pass_send.at[which, n], pass_recv.at[which, n],
                address("row", member("row", move)),
            )

        def across(n, move):
            at = gathered.at[stage, rows_of(member("row", back("row", move)))]
            return remote(at, at, pass_send.at[which, 7 + n], pass_recv.at[which, 7 + n], sibling)

        gathered[stage, rows_of(row)] = outgoing[stage]
        across(7, (0, 0, 0)).start()
        for n, move in enumerate(PLANE_MOVES):
            copy(n, move).start()

        def wait():
            for n, move in reversed(list(enumerate(PLANE_MOVES))):
                at = gathered.at[stage, rows_of(member("row", back("row", move)))]
                remote(at, at, pass_send.at[which, n], pass_recv.at[which, n], here).wait_recv()
                across(n, move).start()
            for n in range(8):
                move = PLANE_MOVES[n] if n < 7 else (0, 0, 0)
                at = gathered.at[stage, rows_of(row + 1 - 2 * core)]
                remote(at, at, pass_send.at[which, n], pass_recv.at[which, 7 + n], here).wait_recv()
            for n, move in enumerate(PLANE_MOVES):
                copy(n, move).wait_send()
                across(n, move).wait_send()
            across(7, (0, 0, 0)).wait_send()

        return wait

    def sum_start(stage, axis):
        for n, move in enumerate(ROW_MOVES if axis == "row" else COL_MOVES):
            to = member(axis, move)
            remote(
                partial.at[stage, rows_of(to)], arrived.at[stage, n], sum_send.at[stage], sum_recv.at[stage],
                address(axis, to),
            ).start()

    def sum_wait(stage):
        every = arrived.at[stage]
        remote(every, every, sum_send.at[stage], sum_recv.at[stage], here).wait()

    centre = jnp.where(row == col, CENTER, 0.0).astype(f32)
    for stage in range(DEGREES):
        over = "row" if stage % 2 == 0 else "col"
        me = row if over == "row" else col
        if stage == 0:
            vectors = left[half, :, :, :, ZONE:].reshape(1024, 128)
        else:
            wait = gather_col(stage) if stage % 2 == 0 else gather_row(stage)
            wait()
            vectors = gathered[stage]
        if stage % 2 == 0:
            image = jnp.dot(vectors.T, tile[...], preferred_element_type=f32).T
        else:
            image = jnp.dot(tile[...], vectors, preferred_element_type=f32)
        image = image - centre * vectors.astype(f32)
        partial[stage] = image.astype(bf16)
        whole[...] = image
        sum_start(stage, over)
        own = whole[rows_of(me)]
        sum_wait(stage)
        total = own + jnp.sum(arrived[stage].astype(f32), axis=0)
        if stage == 0:
            following = total / HALF_WIDTH
        else:
            following = 2.0 / HALF_WIDTH * total - (start[...] if stage == 1 else history[stage - 2])
        if stage < DEGREES - 1:
            outgoing[stage + 1] = following.astype(bf16)
            history[stage] = following
        else:
            filtered[...] = following

    last = pltpu.make_async_copy(filtered, filtered_out, tcc_sem.at[6])
    last.start()

    for q in (1, 2, 3):
        quad(q).wait_send()

    @pl.when(kind != z)
    def _():
        turn().wait_send()

    for way in (0, 1):
        for step, q in in_flight[way]:
            ring(way, step, q).wait_send()
    piece_sent()
    store.wait()
    last.wait()


def on_device(tcc_before, shift_panel, source_map, pixels, start_vectors):
    anywhere = pl.BlockSpec(memory_space=pl.ANY)
    dma = pltpu.SemaphoreType.DMA
    return pl.pallas_call(
        body,
        out_shape=(
            jax.ShapeDtypeStruct(start_vectors.shape, f32),
            jax.ShapeDtypeStruct(tcc_before.shape, bf16),
        ),
        in_specs=[anywhere] * 5,
        out_specs=(anywhere, anywhere),
        scratch_shapes=[
            pltpu.VMEM((ROWS, 512), bf16),
            pltpu.VMEM((1, 1024), f32),
            pltpu.VMEM((1, 512), jnp.int32),
            pltpu.VMEM((ROWS, 128), f32),
            pltpu.VMEM((ROWS, 128), f32),
            pltpu.VMEM((2, 2, 8, ROWS, ZONE + 128), bf16),
            pltpu.VMEM((2, 2, 8, ROWS, ZONE), bf16),
            pltpu.VMEM((1024, 1024), bf16),
            pltpu.VMEM((DEGREES, 1024, 128), bf16),
            pltpu.VMEM((DEGREES, 1024, 128), bf16),
            pltpu.VMEM((DEGREES, N - 1, ROWS, 128), bf16),
            pltpu.VMEM((DEGREES, ROWS, 128), bf16),
            pltpu.VMEM((1024, 128), f32),
            pltpu.VMEM((DEGREES - 1, ROWS, 128), f32),
            dma((7,)), dma((4,)), dma((4,)), dma((2, 4, 4)), dma((2, 4, 4)), dma((1,)),
            dma((4, 4, 7)), dma((2, 2, 8)), dma((DEGREES,)), dma((DEGREES,)), dma((2, 15)), dma((2, 15)),
            dma((DEGREES,)), dma((DEGREES,)),
        ],
        compiler_params=pltpu.CompilerParams(
            collective_id=0, has_side_effects=True, vmem_limit_bytes=60 * 1024 * 1024
        ),
    )(tcc_before, shift_panel, source_map.reshape(1, -1), pixels.reshape(1, -1), start_vectors)


def solution(mesh):
    in_specs = (P("row", "col"), P(("row", "col"), None), P(), P(), P(("row", "col"), None))
    out_specs = (P(("row", "col"), None), P("row", "col"))
    return jax.shard_map(
        on_device, mesh=mesh, in_specs=in_specs, out_specs=out_specs, check_vma=False
    )
```

```python
import jax
import jax.numpy as jnp
from jax import lax
from jax.experimental import pallas as pl
from jax.experimental.pallas import tpu as pltpu
from jax.sharding import PartitionSpec as P

DEGREES = 4
CENTER = 0.45
HALF_WIDTH = 1.6
MESH = pl.DeviceIdType.MESH
N = 16
ROWS = 64
ZONE = 512
WINDOW = 2


def farthest_first(moves, hops):
    return sorted(moves, key=lambda move: -hops(*move))


ROW_MOVES = farthest_first(
    [(dx, dy, dk) for dx in (2, 1, -1, 0) for dy in (1, 0) for dk in (1, 0) if dx or dy or dk],
    lambda dx, dy, dk: abs(dx) + dy,
)
NEAR = (2, -2, 1, -1)
OTHERS = ((1, 3), (1, -3), (0, 4), (0, 3), (0, -3), (1, 0))
PLANE_MOVES = [move for move in ROW_MOVES if move[2] == 0]
f32 = jnp.float32
bf16 = jnp.bfloat16


def mod(value, size):
    return lax.rem(value + size, size)


def device(x, y, core, z):
    x, y, z = mod(x, 4), mod(y, 4), mod(z, 8)
    return (4 * x + 2 * lax.rem(y, 2) + core, 8 * (y // 2) + z)


def body(
    before, panel_in, source_in, pixels_in, start_in, filtered, tile,
    panel, source, pixels, start, left, right, gathered, partial, arrived, outgoing,
    whole, history, crossed, joined,
    tcc_sem, quad_send, quad_recv, ring_send, ring_recv, turn_send,
    piece_send, piece_recv, gather_send, gather_recv, pass_send, pass_recv, sum_send, sum_recv, cross_recv,
):
    row, col = lax.axis_index("row"), lax.axis_index("col")
    x, y_lo, core = row // 4, lax.rem(row // 2, 2), lax.rem(row, 2)
    y_hi, z = col // 8, lax.rem(col, 8)
    y = 2 * y_hi + y_lo
    half = x // 2
    kind = lax.rem(row, 8)
    here = (row, col)
    sibling = (row + 1 - 2 * core, col)

    loads = [
        pltpu.make_async_copy(src, dst, tcc_sem.at[1 + i])
        for i, (src, dst) in enumerate(
            ((pixels_in, pixels), (source_in, source), (panel_in, panel), (start_in, start))
        )
    ]
    for small in loads:
        small.start()
    load = pltpu.make_async_copy(before, tile, tcc_sem.at[0])
    load.start()

    barrier = pltpu.get_barrier_semaphore()

    @pl.loop(1, N)
    def _(step):
        pl.semaphore_signal(barrier, 1, device_id=(mod(row + step, N), col), device_id_type=MESH)
        pl.semaphore_signal(barrier, 1, device_id=(row, mod(col + step, N)), device_id_type=MESH)

    far = jnp.where(y_lo == 0, y - 1, y + 1)
    swapped = (8 * half + z, 8 * y_hi + kind)
    for to in (device(x, far + 4, core, z), device(x + 2, y + 2, core, z), swapped):
        pl.semaphore_signal(barrier, 1, device_id=to, device_id_type=MESH)

    for small in loads:
        small.wait()
    src = jnp.broadcast_to(source[...], (N, source.shape[1]))
    high = src.astype(bf16).astype(f32)
    middle = (src - high).astype(bf16).astype(f32)
    low = src - high - middle
    part = lax.broadcasted_iota(jnp.int32, src.shape, 0)
    parts = jnp.where(part == 0, high, jnp.where(part == 1, middle, jnp.where(part == 2, low, 0.0)))
    place = lax.broadcasted_iota(jnp.int32, (source.shape[1], pixels.shape[1]), 0)
    hit = jnp.where(place == pixels[...], 1.0, 0.0).astype(bf16)
    three = jnp.dot(parts.astype(bf16), hit, preferred_element_type=f32)
    weight = three[0:1] + three[1:2] + three[2:3]
    scaled = (panel[...].astype(f32) * jnp.sqrt(weight)).astype(bf16)
    left[half, y_hi, z, :, :ZONE] = scaled
    left[half, y_hi, z, :, ZONE:] = start[...].astype(bf16)

    @pl.when(kind == z)
    def _():
        right[half, y_hi, z] = scaled

    pl.semaphore_wait(barrier, 2 * (N - 1) + 3)

    def remote(src_ref, dst_ref, send, recv, to):
        return pltpu.make_async_remote_copy(
            src_ref=src_ref, dst_ref=dst_ref, send_sem=send, recv_sem=recv, device_id=to, device_id_type=MESH
        )

    def turn():
        return remote(
            left.at[half, y_hi, z, :, pl.ds(0, ZONE)], right.at[half, y_hi, z], turn_send.at[0],
            piece_recv.at[half, y_hi, z], swapped,
        )

    @pl.when(kind != z)
    def _():
        turn().start()

    def chip(i, j):
        along_x, along_y = jnp.where(core == 0, i, j), jnp.where(core == 0, j, i)
        return mod(x + along_x, 4), mod(y + along_y, 4)

    def place_of(cx, cy, k):
        return cx // 2, cy // 2, 4 * lax.rem(cx, 2) + 2 * lax.rem(cy, 2) + k

    def piece_copy(i, j, way):
        at = place_of(*chip(i, j), core)
        if way is None:
            index, to = 6, sibling
        else:
            tx, ty = chip(*way)
            index, to = (way[0] or 3 + way[1]) - 1, device(tx, ty, core, z)
        return remote(right.at[at], right.at[at], piece_send.at[i, j, index], piece_recv.at[at], to)

    def piece_wait(i, j, k=None):
        cx, cy = chip(i, j)
        at = place_of(cx, cy, core if k is None else k)
        remote(right.at[at], right.at[at], turn_send.at[0], piece_recv.at[at], here).wait_recv()

    def piece_first():
        @pl.when(kind != z)
        def _():
            piece_wait(0, 0)

        for d in (2, 1, 3):
            piece_copy(0, 0, (d, 0)).start()
        for d in (2, 1, 3):
            piece_copy(0, 0, (0, d)).start()
        piece_copy(0, 0, None).start()

    def piece_second():
        for i in (1, 3, 2):
            piece_wait(i, 0)
            for d in (2, 1, 3):
                piece_copy(i, 0, (0, d)).start()
            piece_copy(i, 0, None).start()

    def piece_third():
        for i in (0, 1, 3, 2):
            for j in (1, 3, 2):
                piece_wait(i, j)
                piece_copy(i, j, None).start()

    def piece_last():
        for i in range(4):
            for j in range(4):
                piece_wait(i, j, 1 - core)

    def piece_sent():
        for i in range(4):
            for j in range(4):
                piece_copy(i, j, None).wait_send()
                if j == 0:
                    for d in (1, 2, 3):
                        piece_copy(i, 0, (0, d)).wait_send()
                        if i == 0:
                            piece_copy(0, 0, (d, 0)).wait_send()

    def piece_of(q, zz):
        h, yh = mod(half + q % 2, 2), mod(y_hi + q // 2, 2)
        return left.at[h, yh, zz] if q % 2 == 0 else left.at[h, yh, zz, :, pl.ds(0, ZONE)]

    def quad(q):
        own = left.at[half, y_hi, z]
        own = own if q % 2 == 0 else left.at[half, y_hi, z, :, pl.ds(0, ZONE)]
        return remote(own, own, quad_send.at[q], quad_recv.at[q], device(x + 2 * (q % 2), y + 2 * (q // 2), core, z))

    def quad_wait(q):
        there = piece_of(q, z)
        remote(there, there, quad_send.at[q], quad_recv.at[q], here).wait_recv()

    def ring(way, step, q):
        at = piece_of(q, mod(z - step if way == 0 else z + step, 8))
        return remote(
            at, at, ring_send.at[way, step, q], ring_recv.at[way, step, q],
            device(x, y, core, z + 1 if way == 0 else z + 7),
        )

    def ring_wait(way, step, q):
        at = piece_of(q, mod(z - step - 1 if way == 0 else z + step + 1, 8))
        remote(at, at, ring_send.at[way, step, q], ring_recv.at[way, step, q], here).wait_recv()

    in_flight = [[], []]

    def ring_start(way, step, q):
        if len(in_flight[way]) == WINDOW:
            ring(way, *in_flight[way].pop(0)).wait_send()
        ring(way, step, q).start()
        in_flight[way].append((step, q))

    def ring_step(step):
        for q in range(4):
            if step == 0 and q > 0:
                quad_wait(q)
            for way in (0, 1):
                if step > 0:
                    ring_wait(way, step - 1, q)
                if step < 3 or (q < 2) == (way == 0):
                    ring_start(way, step, q)

    for q in (1, 2, 3):
        quad(q).start()
    ring_step(0)
    piece_first()
    ring_step(1)
    piece_second()
    ring_step(2)
    piece_third()
    ring_step(3)
    piece_last()
    load.wait()

    sign = jnp.where(half == y_hi, 1.0, -1.0).astype(f32)
    nt = (((1,), (1,)), ((), ()))

    def update(yh, quarter):
        zs = pl.ds(4 * quarter, 4)
        span = pl.ds(pl.multiple_of(512 * yh + 256 * quarter, 256), 256)
        straight = lax.dot_general(
            left[half, yh, zs, :, :ZONE].reshape(256, ZONE), right[y_hi].reshape(1024, ZONE), nt,
            preferred_element_type=f32,
        )
        turned = lax.dot_general(
            left[1 - half, yh, zs, :, :ZONE].reshape(256, ZONE), right[1 - y_hi].reshape(1024, ZONE), nt,
            preferred_element_type=f32,
        )
        tile[span] = (tile[span].astype(f32) + (straight + sign * turned)).astype(bf16)

    @pl.loop(0, 2)
    def _(yh):
        update(yh, z // 4)

    for q in range(4):
        for way in (0, 1):
            if (q < 2) == (way == 0):
                ring_wait(way, 3, q)

    @pl.loop(0, 2)
    def _(yh):
        update(yh, 1 - z // 4)

    def member(axis, move):
        if axis == "row":
            dx, dy, dk = move
            return 4 * mod(x + dx, 4) + 2 * mod(y_lo + dy, 2) + mod(core + dk, 2)
        dy, dz = move
        return 8 * mod(y_hi + dy, 2) + mod(z + dz, 8)

    def back(axis, move):
        return tuple(-d for d in move)

    def address(axis, index):
        return (index, col) if axis == "row" else (row, index)

    def rows_of(index):
        return pl.ds(pl.multiple_of(index * ROWS, ROWS), ROWS)

    def piece_ref(stage, index):
        return partial.at[stage, index // 2, lax.rem(index, 2)]

    partner = (row, member("col", (1, 0)))

    def gather_col(stage):
        at = gathered.at[stage, rows_of(col)]
        gathered[stage, rows_of(col)] = outgoing[stage]

        def copy(recv, move):
            remote(outgoing.at[stage], at, gather_send.at[0], recv, address("col", member("col", move))).start()

        copy(gather_recv.at[4], (1, 4))
        for n, dz in enumerate(NEAR):
            copy(gather_recv.at[n], (0, dz))
        for move in OTHERS:
            copy(gather_recv.at[4], move)

        def wait():
            for n, dz in reversed(list(enumerate(NEAR))):
                near = gathered.at[stage, rows_of(member("col", (0, -dz)))]
                remote(near, near, gather_send.at[0], gather_recv.at[n], here).wait_recv()
                remote(near, near, gather_send.at[0], gather_recv.at[4], partner).start()
            rest = gathered.at[stage, pl.ds(0, 11 * ROWS)]
            remote(rest, rest, gather_send.at[0], gather_recv.at[4], here).wait_recv()
            sent = gathered.at[stage, pl.ds(0, 15 * ROWS)]
            remote(sent, sent, gather_send.at[0], gather_recv.at[4], here).wait_send()

        return wait

    def gather_row(stage):
        which = stage // 2

        def copy(n, move):
            at = gathered.at[stage, rows_of(row)]
            return remote(
                outgoing.at[stage], at, pass_send.at[which, n], pass_recv.at[which, n],
                address("row", member("row", move)),
            )

        def across(n, move):
            at = gathered.at[stage, rows_of(member("row", back("row", move)))]
            return remote(at, at, pass_send.at[which, 7 + n], pass_recv.at[which, 7 + n], sibling)

        gathered[stage, rows_of(row)] = outgoing[stage]
        across(7, (0, 0, 0)).start()
        for n, move in enumerate(PLANE_MOVES):
            copy(n, move).start()

        def wait():
            for n, move in reversed(list(enumerate(PLANE_MOVES))):
                at = gathered.at[stage, rows_of(member("row", back("row", move)))]
                remote(at, at, pass_send.at[which, n], pass_recv.at[which, n], here).wait_recv()
                across(n, move).start()
            for n in range(8):
                move = PLANE_MOVES[n] if n < 7 else (0, 0, 0)
                at = gathered.at[stage, rows_of(row + 1 - 2 * core)]
                remote(at, at, pass_send.at[which, n], pass_recv.at[which, 7 + n], here).wait_recv()
            for n, move in enumerate(PLANE_MOVES):
                copy(n, move).wait_send()
                across(n, move).wait_send()
            across(7, (0, 0, 0)).wait_send()

        return wait

    def all_sent(stage):
        every = arrived.at[stage]
        remote(every, every, sum_send.at[stage], sum_recv.at[stage], here).wait_send()

    def sum_row(stage):
        which = stage // 2
        theirs = partial.at[stage, :, 1 - core]
        remote(theirs, crossed.at[which], sum_send.at[stage], cross_recv.at[which], sibling).start()
        remote(theirs, crossed.at[which], sum_send.at[stage], cross_recv.at[which], here).wait_recv()
        both = whole[:, core] + crossed[which].astype(f32)
        joined[which] = both.astype(bf16)
        whole[:, core] = both
        for n, move in enumerate(PLANE_MOVES):
            to = member("row", move)
            remote(
                joined.at[which, to // 2], arrived.at[stage, n], sum_send.at[stage], sum_recv.at[stage],
                address("row", to),
            ).start()
        if stage == 0:
            panels_sent()
        mine = whole[row // 2, core]
        every = arrived.at[stage, pl.ds(0, 7)]
        remote(every, every, sum_send.at[stage], sum_recv.at[stage], here).wait_recv()
        all_sent(stage)
        return mine + jnp.sum(arrived[stage, :7].astype(f32), axis=0)

    def sum_col(stage):
        which = 2 + stage // 2

        def copy(src, slot, move):
            remote(
                src, arrived.at[stage, slot], sum_send.at[stage], sum_recv.at[stage], address("col", member("col", move))
            ).start()

        copy(piece_ref(stage, member("col", (1, 4))), 0, (1, 4))
        for n, dz in enumerate(NEAR):
            remote(
                piece_ref(stage, member("col", (1, dz))), crossed.at[which, n], sum_send.at[stage],
                cross_recv.at[which], partner,
            ).start()
        for n, move in enumerate(OTHERS):
            copy(piece_ref(stage, member("col", move)), 1 + n, move)
        some = crossed.at[which, pl.ds(0, 4)]
        remote(some, some, sum_send.at[stage], cross_recv.at[which], here).wait_recv()
        for n, dz in enumerate(NEAR):
            to = member("col", (0, dz))
            joined[which, n] = (whole[to // 2, lax.rem(to, 2)] + crossed[which, n].astype(f32)).astype(bf16)
            copy(joined.at[which, n], 7 + n, (0, dz))
        mine = whole[col // 2, lax.rem(col, 2)]
        every = arrived.at[stage, pl.ds(0, 11)]
        remote(every, every, sum_send.at[stage], sum_recv.at[stage], here).wait_recv()
        all_sent(stage)
        return mine + jnp.sum(arrived[stage, :11].astype(f32), axis=0)

    def panels_sent():
        for q in (1, 2, 3):
            quad(q).wait_send()

        @pl.when(kind != z)
        def _():
            turn().wait_send()

        for way in (0, 1):
            for step, q in in_flight[way]:
                ring(way, step, q).wait_send()
        piece_sent()

    centre = jnp.where(row == col, CENTER, 0.0).astype(f32)
    for stage in range(DEGREES):
        if stage == 0:
            vectors = left[half, :, :, :, ZONE:].reshape(1024, 128)
        else:
            wait = gather_col(stage) if stage % 2 == 0 else gather_row(stage)
            wait()
            vectors = gathered[stage]
        if stage % 2 == 0:
            image = jnp.dot(vectors.T, tile[...], preferred_element_type=f32).T
        else:
            image = jnp.dot(tile[...], vectors, preferred_element_type=f32)
        image = image - centre * vectors.astype(f32)
        partial[stage] = image.astype(bf16).reshape(8, 2, ROWS, 128)
        whole[...] = image.reshape(8, 2, ROWS, 128)
        total = sum_row(stage) if stage % 2 == 0 else sum_col(stage)
        if stage == 0:
            following = total / HALF_WIDTH
        else:
            following = 2.0 / HALF_WIDTH * total - (start[...] if stage == 1 else history[stage - 2])
        if stage < DEGREES - 1:
            outgoing[stage + 1] = following.astype(bf16)
            history[stage] = following
        else:
            filtered[...] = following


def on_device(tcc_before, shift_panel, source_map, pixels, start_vectors):
    hbm = pl.BlockSpec(memory_space=pltpu.HBM)
    vmem = pl.BlockSpec(memory_space=pltpu.VMEM)
    dma = pltpu.SemaphoreType.DMA
    operands = (tcc_before, shift_panel, source_map.reshape(1, -1), pixels.reshape(1, -1), start_vectors)
    operands = [pltpu.with_memory_space_constraint(operand, pltpu.HBM) for operand in operands]
    return pl.pallas_call(
        body,
        out_shape=(
            jax.ShapeDtypeStruct(start_vectors.shape, f32),
            jax.ShapeDtypeStruct(tcc_before.shape, bf16),
        ),
        in_specs=[hbm] * 5,
        out_specs=(vmem, vmem),
        scratch_shapes=[
            pltpu.VMEM((ROWS, 512), bf16),
            pltpu.VMEM((1, 1024), f32),
            pltpu.VMEM((1, 512), jnp.int32),
            pltpu.VMEM((ROWS, 128), f32),
            pltpu.VMEM((2, 2, 8, ROWS, ZONE + 128), bf16),
            pltpu.VMEM((2, 2, 8, ROWS, ZONE), bf16),
            pltpu.VMEM((DEGREES, 1024, 128), bf16),
            pltpu.VMEM((DEGREES, 8, 2, ROWS, 128), bf16),
            pltpu.VMEM((DEGREES, N - 1, ROWS, 128), bf16),
            pltpu.VMEM((DEGREES, ROWS, 128), bf16),
            pltpu.VMEM((8, 2, ROWS, 128), f32),
            pltpu.VMEM((DEGREES - 1, ROWS, 128), f32),
            pltpu.VMEM((DEGREES, 8, ROWS, 128), bf16),
            pltpu.VMEM((DEGREES, 8, ROWS, 128), bf16),
            dma((5,)), dma((4,)), dma((4,)), dma((2, 4, 4)), dma((2, 4, 4)), dma((1,)),
            dma((4, 4, 7)), dma((2, 2, 8)), dma((1,)), dma((5,)), dma((2, 15)), dma((2, 15)),
            dma((DEGREES,)), dma((DEGREES,)), dma((DEGREES,)),
        ],
        compiler_params=pltpu.CompilerParams(
            collective_id=0, has_side_effects=True, vmem_limit_bytes=32 * 1024 * 1024
        ),
    )(*operands)


def solution(mesh):
    in_specs = (P("row", "col"), P(("row", "col"), None), P(), P(), P(("row", "col"), None))
    out_specs = (P(("row", "col"), None), P("row", "col"))
    return jax.shard_map(
        on_device, mesh=mesh, in_specs=in_specs, out_specs=out_specs, check_vma=False
    )
```

```python
import jax
import jax.numpy as jnp
from jax import lax
from jax.experimental import pallas as pl
from jax.experimental.pallas import tpu as pltpu
from jax.sharding import PartitionSpec as P

DEGREES = 4
CENTER = 0.45
HALF_WIDTH = 1.6
MESH = pl.DeviceIdType.MESH
N = 16
ROWS = 64
ZONE = 512
WINDOW = 4


def farthest_first(moves, hops):
    return sorted(moves, key=lambda move: -hops(*move))


MOVES = {
    "row": farthest_first(
        [(dx, dy, dk) for dx in (2, 1, -1, 0) for dy in (1, 0) for dk in (1, 0) if dx or dy or dk],
        lambda dx, dy, dk: abs(dx) + dy,
    ),
    "col": farthest_first(
        [(dy, dz) for dy in (1, 0) for dz in (4, 3, -3, 2, -2, 1, -1, 0) if dy or dz],
        lambda dy, dz: 2 * dy + abs(dz),
    ),
}
f32 = jnp.float32
bf16 = jnp.bfloat16


def mod(value, size):
    return lax.rem(value + size, size)


def device(x, y, core, z):
    x, y, z = mod(x, 4), mod(y, 4), mod(z, 8)
    return (4 * x + 2 * lax.rem(y, 2) + core, 8 * (y // 2) + z)


def body(
    before, panel_in, source_in, pixels_in, start_in, filtered, tile,
    panel, source, pixels, start, left, right, gathered, partial, arrived, outgoing,
    whole, history,
    tcc_sem, quad_send, quad_recv, ring_send, ring_recv, turn_send,
    piece_send, piece_recv, relay_send, relay_recv, gather_send, gather_recv, sum_send, sum_recv,
):
    row, col = lax.axis_index("row"), lax.axis_index("col")
    x, y_lo, core = row // 4, lax.rem(row // 2, 2), lax.rem(row, 2)
    y_hi, z = col // 8, lax.rem(col, 8)
    y = 2 * y_hi + y_lo
    half = x // 2
    kind = lax.rem(row, 8)
    here = (row, col)
    sibling = (row + 1 - 2 * core, col)

    loads = [
        pltpu.make_async_copy(src, dst, tcc_sem.at[1 + i])
        for i, (src, dst) in enumerate(
            ((pixels_in, pixels), (source_in, source), (panel_in, panel), (start_in, start))
        )
    ]
    for small in loads:
        small.start()
    load = pltpu.make_async_copy(before, tile, tcc_sem.at[0])
    load.start()

    barrier = pltpu.get_barrier_semaphore()

    @pl.loop(1, N)
    def _(step):
        pl.semaphore_signal(barrier, 1, device_id=(mod(row + step, N), col), device_id_type=MESH)
        pl.semaphore_signal(barrier, 1, device_id=(row, mod(col + step, N)), device_id_type=MESH)

    far = jnp.where(y_lo == 0, y - 1, y + 1)
    swapped = (8 * half + z, 8 * y_hi + kind)
    for to in (device(x, far + 4, core, z), device(x + 2, y + 2, core, z), swapped):
        pl.semaphore_signal(barrier, 1, device_id=to, device_id_type=MESH)

    for small in loads:
        small.wait()
    src = jnp.broadcast_to(source[...], (N, source.shape[1]))
    high = src.astype(bf16).astype(f32)
    middle = (src - high).astype(bf16).astype(f32)
    low = src - high - middle
    part = lax.broadcasted_iota(jnp.int32, src.shape, 0)
    parts = jnp.where(part == 0, high, jnp.where(part == 1, middle, jnp.where(part == 2, low, 0.0)))
    place = lax.broadcasted_iota(jnp.int32, (source.shape[1], pixels.shape[1]), 0)
    hit = jnp.where(place == pixels[...], 1.0, 0.0).astype(bf16)
    three = jnp.dot(parts.astype(bf16), hit, preferred_element_type=f32)
    weight = three[0:1] + three[1:2] + three[2:3]
    scaled = (panel[...].astype(f32) * jnp.sqrt(weight)).astype(bf16)
    left[half, y_hi, z, :, :ZONE] = scaled
    left[half, y_hi, z, :, ZONE:] = start[...].astype(bf16)

    @pl.when(kind == z)
    def _():
        right[half, y_hi, z] = scaled

    pl.semaphore_wait(barrier, 2 * (N - 1) + 3)

    def remote(src_ref, dst_ref, send, recv, to):
        return pltpu.make_async_remote_copy(
            src_ref=src_ref, dst_ref=dst_ref, send_sem=send, recv_sem=recv, device_id=to, device_id_type=MESH
        )

    def turn():
        return remote(
            left.at[half, y_hi, z, :, pl.ds(0, ZONE)], right.at[half, y_hi, z], turn_send.at[0],
            piece_recv.at[half, y_hi, z], swapped,
        )

    @pl.when(kind != z)
    def _():
        turn().start()

    def chip(i, j):
        along_x, along_y = jnp.where(core == 0, i, j), jnp.where(core == 0, j, i)
        return mod(x + along_x, 4), mod(y + along_y, 4)

    def place_of(cx, cy, k):
        return cx // 2, cy // 2, 4 * lax.rem(cx, 2) + 2 * lax.rem(cy, 2) + k

    def piece_copy(i, j, way):
        at = place_of(*chip(i, j), core)
        if way is None:
            index, to = 6, sibling
        else:
            tx, ty = chip(*way)
            index, to = (way[0] or 3 + way[1]) - 1, device(tx, ty, core, z)
        return remote(right.at[at], right.at[at], piece_send.at[i, j, index], piece_recv.at[at], to)

    def piece_wait(i, j, k=None):
        cx, cy = chip(i, j)
        at = place_of(cx, cy, core if k is None else k)
        remote(right.at[at], right.at[at], turn_send.at[0], piece_recv.at[at], here).wait_recv()

    def piece_first():
        @pl.when(kind != z)
        def _():
            piece_wait(0, 0)

        for d in (2, 1, 3):
            piece_copy(0, 0, (d, 0)).start()
        for d in (2, 1, 3):
            piece_copy(0, 0, (0, d)).start()
        piece_copy(0, 0, None).start()

    def piece_second():
        for i in (1, 3, 2):
            piece_wait(i, 0)
            for d in (2, 1, 3):
                piece_copy(i, 0, (0, d)).start()
            piece_copy(i, 0, None).start()

    def piece_third():
        for i in (0, 1, 3, 2):
            for j in (1, 3, 2):
                piece_wait(i, j)
                piece_copy(i, j, None).start()

    def piece_last():
        for i in range(4):
            for j in range(4):
                piece_wait(i, j, 1 - core)

    def piece_sent():
        for i in range(4):
            for j in range(4):
                piece_copy(i, j, None).wait_send()
                if j == 0:
                    for d in (1, 2, 3):
                        piece_copy(i, 0, (0, d)).wait_send()
                        if i == 0:
                            piece_copy(0, 0, (d, 0)).wait_send()

    def piece_of(q, zz):
        h, yh = mod(half + q % 2, 2), mod(y_hi + q // 2, 2)
        return left.at[h, yh, zz] if q % 2 == 0 else left.at[h, yh, zz, :, pl.ds(0, ZONE)]

    def quad(q):
        own = left.at[half, y_hi, z]
        own = own if q % 2 == 0 else left.at[half, y_hi, z, :, pl.ds(0, ZONE)]
        return remote(own, own, quad_send.at[q], quad_recv.at[q], device(x + 2 * (q % 2), y + 2 * (q // 2), core, z))

    def quad_wait(q):
        there = piece_of(q, z)
        remote(there, there, quad_send.at[q], quad_recv.at[q], here).wait_recv()

    def travelling(q, zz):
        if q == 1:
            return left.at[1 - half, y_hi, zz, pl.ds(0, 32), pl.ds(0, ZONE)]
        if q == 2:
            return left.at[half, 1 - y_hi, zz, pl.ds(0, 32)]
        return piece_of(q, zz)

    def relay(way, step, q, arriving):
        h, yh = (half, y_hi) if not arriving else (1 - half, y_hi) if q == 1 else (half, 1 - y_hi)
        zz, upper = mod(z - step - 1 if way == 0 else z + step + 1, 8), pl.ds(32, 32)
        at = left.at[h, yh, zz, upper, pl.ds(0, ZONE)] if q == 1 else left.at[h, yh, zz, upper]
        to = here if arriving else device(x + 2 * (q % 2), y + 2 * (q // 2), core, z)
        return remote(at, at, relay_send.at[way, step, q - 1], relay_recv.at[way, step, q - 1], to)

    def ring(way, step, q):
        at = travelling(q, mod(z - step if way == 0 else z + step, 8))
        return remote(
            at, at, ring_send.at[way, step, q], ring_recv.at[way, step, q],
            device(x, y, core, z + 1 if way == 0 else z + 7),
        )

    def ring_wait(way, step, q):
        at = travelling(q, mod(z - step - 1 if way == 0 else z + step + 1, 8))
        remote(at, at, ring_send.at[way, step, q], ring_recv.at[way, step, q], here).wait_recv()
        if q == 0:
            for partner in (1, 2):
                relay(way, step, partner, False).start()

    in_flight = [[], []]

    def ring_start(way, step, q):
        if len(in_flight[way]) == WINDOW:
            ring(way, *in_flight[way].pop(0)).wait_send()
        ring(way, step, q).start()
        in_flight[way].append((step, q))

    def ring_go(step, q):
        if step == 0 and q > 0:
            quad_wait(q)
        for way in (0, 1):
            if step > 0:
                ring_wait(way, step - 1, q)
            if step < 3 or (q < 2) == (way == 0):
                ring_start(way, step, q)

    for q in (1, 2, 3):
        quad(q).start()
    for q in range(4):
        ring_go(0, q)
    piece_first()
    for q in range(4):
        ring_go(1, q)
    piece_second()
    for q in range(4):
        ring_go(2, q)
    for q in range(4):
        ring_go(3, q)
    piece_third()
    piece_last()
    load.wait()
    for step in range(3):
        for way in (0, 1):
            for partner in (1, 2):
                relay(way, step, partner, True).wait_recv()

    sign = jnp.where(half == y_hi, 1.0, -1.0).astype(f32)
    nt = (((1,), (1,)), ((), ()))

    def update(yh, quarter):
        zs = pl.ds(4 * quarter, 4)
        span = pl.ds(pl.multiple_of(512 * yh + 256 * quarter, 256), 256)
        straight = lax.dot_general(
            left[half, yh, zs, :, :ZONE].reshape(256, ZONE), right[y_hi].reshape(1024, ZONE), nt,
            preferred_element_type=f32,
        )
        turned = lax.dot_general(
            left[1 - half, yh, zs, :, :ZONE].reshape(256, ZONE), right[1 - y_hi].reshape(1024, ZONE), nt,
            preferred_element_type=f32,
        )
        tile[span] = (tile[span].astype(f32) + (straight + sign * turned)).astype(bf16)

    ring_wait(0, 3, 0)

    @pl.loop(0, 2)
    def _(yh):
        update(yh, z // 4)

    for way, q in ((1, 2), (0, 1), (1, 3)):
        ring_wait(way, 3, q)
    for partner in (1, 2):
        relay(0, 3, partner, True).wait_recv()

    @pl.loop(0, 2)
    def _(yh):
        update(yh, 1 - z // 4)

    def member(axis, move):
        if axis == "row":
            dx, dy, dk = move
            return 4 * mod(x + dx, 4) + 2 * mod(y_lo + dy, 2) + mod(core + dk, 2)
        dy, dz = move
        return 8 * mod(y_hi + dy, 2) + mod(z + dz, 8)

    def address(axis, index):
        return (index, col) if axis == "row" else (row, index)

    def rows_of(index):
        return pl.ds(pl.multiple_of(index * ROWS, ROWS), ROWS)

    def gather(stage, axis):
        me = row if axis == "row" else col
        at = gathered.at[stage, rows_of(me)]
        gathered[stage, rows_of(me)] = outgoing[stage]
        for move in MOVES[axis]:
            remote(
                outgoing.at[stage], at, gather_send.at[stage], gather_recv.at[stage], address(axis, member(axis, move))
            ).start()
        every = gathered.at[stage, pl.ds(0, (N - 1) * ROWS)]
        remote(every, every, gather_send.at[stage], gather_recv.at[stage], here).wait()

    def total_of(stage, axis):
        me = row if axis == "row" else col
        for n, move in enumerate(MOVES[axis]):
            to = member(axis, move)
            remote(
                partial.at[stage, rows_of(to)], arrived.at[stage, n], sum_send.at[stage], sum_recv.at[stage],
                address(axis, to),
            ).start()
        if stage == 0:
            panels_sent()
        mine = whole[rows_of(me)]
        every = arrived.at[stage]
        remote(every, every, sum_send.at[stage], sum_recv.at[stage], here).wait()
        return mine + jnp.sum(arrived[stage].astype(f32), axis=0)

    def panels_sent():
        for q in (1, 2, 3):
            quad(q).wait_send()

        @pl.when(kind != z)
        def _():
            turn().wait_send()

        for way in (0, 1):
            for step, q in in_flight[way]:
                ring(way, step, q).wait_send()
            for step in range(4 - way):
                for q in (1, 2):
                    relay(way, step, q, False).wait_send()
        piece_sent()

    centre = jnp.where(row == col, CENTER, 0.0).astype(f32)
    for stage in range(DEGREES):
        if stage == 0:
            vectors = left[half, :, :, :, ZONE:].reshape(1024, 128)
        else:
            gather(stage, "col" if stage % 2 == 0 else "row")
            vectors = gathered[stage]
        if stage % 2 == 0:
            image = jnp.dot(vectors.T, tile[...], preferred_element_type=f32).T
        else:
            image = jnp.dot(tile[...], vectors, preferred_element_type=f32)
        image = image - centre * vectors.astype(f32)
        partial[stage] = image.astype(bf16)
        whole[...] = image
        total = total_of(stage, "row" if stage % 2 == 0 else "col")
        if stage == 0:
            following = total / HALF_WIDTH
        else:
            following = 2.0 / HALF_WIDTH * total - (start[...] if stage == 1 else history[stage - 2])
        if stage < DEGREES - 1:
            outgoing[stage + 1] = following.astype(bf16)
            history[stage] = following
        else:
            filtered[...] = following


def on_device(tcc_before, shift_panel, source_map, pixels, start_vectors):
    hbm = pl.BlockSpec(memory_space=pltpu.HBM)
    vmem = pl.BlockSpec(memory_space=pltpu.VMEM)
    dma = pltpu.SemaphoreType.DMA
    operands = (tcc_before, shift_panel, source_map.reshape(1, -1), pixels.reshape(1, -1), start_vectors)
    operands = [pltpu.with_memory_space_constraint(operand, pltpu.HBM) for operand in operands]
    return pl.pallas_call(
        body,
        out_shape=(
            jax.ShapeDtypeStruct(start_vectors.shape, f32),
            jax.ShapeDtypeStruct(tcc_before.shape, bf16),
        ),
        in_specs=[hbm] * 5,
        out_specs=(vmem, vmem),
        scratch_shapes=[
            pltpu.VMEM((ROWS, 512), bf16),
            pltpu.VMEM((1, 1024), f32),
            pltpu.VMEM((1, 512), jnp.int32),
            pltpu.VMEM((ROWS, 128), f32),
            pltpu.VMEM((2, 2, 8, ROWS, ZONE + 128), bf16),
            pltpu.VMEM((2, 2, 8, ROWS, ZONE), bf16),
            pltpu.VMEM((DEGREES, 1024, 128), bf16),
            pltpu.VMEM((DEGREES, 1024, 128), bf16),
            pltpu.VMEM((DEGREES, N - 1, ROWS, 128), bf16),
            pltpu.VMEM((DEGREES, ROWS, 128), bf16),
            pltpu.VMEM((1024, 128), f32),
            pltpu.VMEM((DEGREES - 1, ROWS, 128), f32),
            dma((5,)), dma((4,)), dma((4,)), dma((2, 4, 4)), dma((2, 4, 4)), dma((1,)),
            dma((4, 4, 7)), dma((2, 2, 8)), dma((2, 4, 2)), dma((2, 4, 2)),
            dma((DEGREES,)), dma((DEGREES,)), dma((DEGREES,)), dma((DEGREES,)),
        ],
        compiler_params=pltpu.CompilerParams(
            collective_id=0, has_side_effects=True, vmem_limit_bytes=32 * 1024 * 1024
        ),
    )(*operands)


def solution(mesh):
    in_specs = (P("row", "col"), P(("row", "col"), None), P(), P(), P(("row", "col"), None))
    out_specs = (P(("row", "col"), None), P("row", "col"))
    return jax.shard_map(
        on_device, mesh=mesh, in_specs=in_specs, out_specs=out_specs, check_vma=False
    )
```

```python
import jax
import jax.numpy as jnp
from jax import lax
from jax.experimental import pallas as pl
from jax.experimental.pallas import tpu as pltpu
from jax.sharding import PartitionSpec as P

DEGREES = 4
CENTER = 0.45
HALF_WIDTH = 1.6
MESH = pl.DeviceIdType.MESH
N = 16
ROWS = 64
ZONE = 512
WINDOW = 4


def farthest_first(moves, hops):
    return sorted(moves, key=lambda move: -hops(*move))


MOVES = {
    "row": farthest_first(
        [(dx, dy, dk) for dx in (2, 1, -1, 0) for dy in (1, 0) for dk in (1, 0) if dx or dy or dk],
        lambda dx, dy, dk: abs(dx) + dy,
    ),
    "col": farthest_first(
        [(dy, dz) for dy in (1, 0) for dz in (4, 3, -3, 2, -2, 1, -1, 0) if dy or dz],
        lambda dy, dz: 2 * dy + abs(dz),
    ),
}
f32 = jnp.float32
bf16 = jnp.bfloat16


def mod(value, size):
    return lax.rem(value + size, size)


def device(x, y, core, z):
    x, y, z = mod(x, 4), mod(y, 4), mod(z, 8)
    return (4 * x + 2 * lax.rem(y, 2) + core, 8 * (y // 2) + z)


def body(
    before, panel_in, source_in, pixels_in, start_in, filtered, tile,
    panel, source, pixels, start, left, right, gathered, partial, arrived, outgoing,
    whole, history,
    tcc_sem, quad_send, quad_recv, ring_send, ring_recv, turn_send,
    piece_send, piece_recv, relay_send, relay_recv, gather_send, gather_recv, sum_send, sum_recv,
):
    row, col = lax.axis_index("row"), lax.axis_index("col")
    x, y_lo, core = row // 4, lax.rem(row // 2, 2), lax.rem(row, 2)
    y_hi, z = col // 8, lax.rem(col, 8)
    y = 2 * y_hi + y_lo
    half = x // 2
    kind = lax.rem(row, 8)
    here = (row, col)
    sibling = (row + 1 - 2 * core, col)

    loads = [
        pltpu.make_async_copy(src, dst, tcc_sem.at[1 + i])
        for i, (src, dst) in enumerate(
            ((pixels_in, pixels), (source_in, source), (panel_in, panel), (start_in, start))
        )
    ]
    for small in loads:
        small.start()
    load = pltpu.make_async_copy(before, tile, tcc_sem.at[0])
    load.start()

    barrier = pltpu.get_barrier_semaphore()

    @pl.loop(1, N)
    def _(step):
        pl.semaphore_signal(barrier, 1, device_id=(mod(row + step, N), col), device_id_type=MESH)
        pl.semaphore_signal(barrier, 1, device_id=(row, mod(col + step, N)), device_id_type=MESH)

    far = jnp.where(y_lo == 0, y - 1, y + 1)
    swapped = (8 * half + z, 8 * y_hi + kind)
    for to in (device(x, far + 4, core, z), device(x + 2, y + 2, core, z), swapped):
        pl.semaphore_signal(barrier, 1, device_id=to, device_id_type=MESH)

    for small in loads:
        small.wait()
    src = jnp.broadcast_to(source[...], (N, source.shape[1]))
    high = src.astype(bf16).astype(f32)
    middle = (src - high).astype(bf16).astype(f32)
    low = src - high - middle
    part = lax.broadcasted_iota(jnp.int32, src.shape, 0)
    parts = jnp.where(part == 0, high, jnp.where(part == 1, middle, jnp.where(part == 2, low, 0.0)))
    place = lax.broadcasted_iota(jnp.int32, (source.shape[1], pixels.shape[1]), 0)
    hit = jnp.where(place == pixels[...], 1.0, 0.0).astype(bf16)
    three = jnp.dot(parts.astype(bf16), hit, preferred_element_type=f32)
    weight = three[0:1] + three[1:2] + three[2:3]
    scaled = (panel[...].astype(f32) * jnp.sqrt(weight)).astype(bf16)
    left[half, y_hi, z, :, :ZONE] = scaled
    left[half, y_hi, z, :, ZONE:] = start[...].astype(bf16)

    @pl.when(kind == z)
    def _():
        right[half, y_hi, z] = scaled

    pl.semaphore_wait(barrier, 2 * (N - 1) + 3)

    def remote(src_ref, dst_ref, send, recv, to):
        return pltpu.make_async_remote_copy(
            src_ref=src_ref, dst_ref=dst_ref, send_sem=send, recv_sem=recv, device_id=to, device_id_type=MESH
        )

    def turn():
        return remote(
            left.at[half, y_hi, z, :, pl.ds(0, ZONE)], right.at[half, y_hi, z], turn_send.at[0],
            piece_recv.at[half, y_hi, z], swapped,
        )

    @pl.when(kind != z)
    def _():
        turn().start()

    def chip(i, j):
        along_x, along_y = jnp.where(core == 0, i, j), jnp.where(core == 0, j, i)
        return mod(x + along_x, 4), mod(y + along_y, 4)

    def place_of(cx, cy, k):
        return cx // 2, cy // 2, 4 * lax.rem(cx, 2) + 2 * lax.rem(cy, 2) + k

    def piece_copy(i, j, way):
        at = place_of(*chip(i, j), core)
        if way is None:
            index, to = 6, sibling
        else:
            tx, ty = chip(*way)
            index, to = (way[0] or 3 + way[1]) - 1, device(tx, ty, core, z)
        return remote(right.at[at], right.at[at], piece_send.at[i, j, index], piece_recv.at[at], to)

    def piece_wait(i, j, k=None):
        cx, cy = chip(i, j)
        at = place_of(cx, cy, core if k is None else k)
        remote(right.at[at], right.at[at], turn_send.at[0], piece_recv.at[at], here).wait_recv()

    def piece_first():
        @pl.when(kind != z)
        def _():
            piece_wait(0, 0)

        for d in (2, 1, 3):
            piece_copy(0, 0, (d, 0)).start()
        for d in (2, 1, 3):
            piece_copy(0, 0, (0, d)).start()
        piece_copy(0, 0, None).start()

    def piece_second():
        for i in (1, 3, 2):
            piece_wait(i, 0)
            for d in (2, 1, 3):
                piece_copy(i, 0, (0, d)).start()
            piece_copy(i, 0, None).start()

    def piece_third():
        for i in (0, 1, 3, 2):
            for j in (1, 3, 2):
                piece_wait(i, j)
                piece_copy(i, j, None).start()

    def piece_last():
        for i in range(4):
            for j in range(4):
                piece_wait(i, j, 1 - core)

    def piece_sent():
        for i in range(4):
            for j in range(4):
                piece_copy(i, j, None).wait_send()
                if j == 0:
                    for d in (1, 2, 3):
                        piece_copy(i, 0, (0, d)).wait_send()
                        if i == 0:
                            piece_copy(0, 0, (d, 0)).wait_send()

    def piece_of(q, zz):
        h, yh = mod(half + q % 2, 2), mod(y_hi + q // 2, 2)
        return left.at[h, yh, zz] if q % 2 == 0 else left.at[h, yh, zz, :, pl.ds(0, ZONE)]

    def quad(q):
        own = left.at[half, y_hi, z]
        own = own if q % 2 == 0 else left.at[half, y_hi, z, :, pl.ds(0, ZONE)]
        return remote(own, own, quad_send.at[q], quad_recv.at[q], device(x + 2 * (q % 2), y + 2 * (q // 2), core, z))

    def quad_wait(q):
        there = piece_of(q, z)
        remote(there, there, quad_send.at[q], quad_recv.at[q], here).wait_recv()

    def travelling(q, zz):
        if q == 1:
            return left.at[1 - half, y_hi, zz, pl.ds(0, 32), pl.ds(0, ZONE)]
        if q == 2:
            return left.at[half, 1 - y_hi, zz, pl.ds(0, 32)]
        return piece_of(q, zz)

    def relay(way, step, q, arriving):
        h, yh = (half, y_hi) if not arriving else (1 - half, y_hi) if q == 1 else (half, 1 - y_hi)
        zz, upper = mod(z - step - 1 if way == 0 else z + step + 1, 8), pl.ds(32, 32)
        at = left.at[h, yh, zz, upper, pl.ds(0, ZONE)] if q == 1 else left.at[h, yh, zz, upper]
        to = here if arriving else device(x + 2 * (q % 2), y + 2 * (q // 2), core, z)
        return remote(at, at, relay_send.at[way, step, q - 1], relay_recv.at[way, step, q - 1], to)

    def ring(way, step, q):
        at = travelling(q, mod(z - step if way == 0 else z + step, 8))
        return remote(
            at, at, ring_send.at[way, step, q], ring_recv.at[way, step, q],
            device(x, y, core, z + 1 if way == 0 else z + 7),
        )

    def ring_wait(way, step, q):
        at = travelling(q, mod(z - step - 1 if way == 0 else z + step + 1, 8))
        remote(at, at, ring_send.at[way, step, q], ring_recv.at[way, step, q], here).wait_recv()
        if q == 0:
            for partner in (1, 2):
                relay(way, step, partner, False).start()

    in_flight = [[], []]

    def ring_start(way, step, q):
        if len(in_flight[way]) == WINDOW:
            ring(way, *in_flight[way].pop(0)).wait_send()
        ring(way, step, q).start()
        in_flight[way].append((step, q))

    def ring_go(step, q):
        if step == 0 and q > 0:
            quad_wait(q)
        for way in (0, 1):
            if step > 0:
                ring_wait(way, step - 1, q)
            if step < 3 or (q < 2) == (way == 0):
                ring_start(way, step, q)

    for q in (1, 2, 3):
        quad(q).start()
    for q in range(4):
        ring_go(0, q)
    piece_first()
    for q in range(4):
        ring_go(1, q)
    piece_second()
    for q in range(4):
        ring_go(2, q)
    for q in range(4):
        ring_go(3, q)
    piece_third()
    piece_last()
    load.wait()
    for step in range(3):
        for way in (0, 1):
            for partner in (1, 2):
                relay(way, step, partner, True).wait_recv()

    sign = jnp.where(half == y_hi, 1.0, -1.0).astype(f32)
    nt = (((1,), (1,)), ((), ()))

    def update(yh, quarter):
        zs = pl.ds(4 * quarter, 4)
        span = pl.ds(pl.multiple_of(512 * yh + 256 * quarter, 256), 256)
        straight = lax.dot_general(
            left[half, yh, zs, :, :ZONE].reshape(256, ZONE), right[y_hi].reshape(1024, ZONE), nt,
            preferred_element_type=f32,
        )
        turned = lax.dot_general(
            left[1 - half, yh, zs, :, :ZONE].reshape(256, ZONE), right[1 - y_hi].reshape(1024, ZONE), nt,
            preferred_element_type=f32,
        )
        tile[span] = (tile[span].astype(f32) + (straight + sign * turned)).astype(bf16)

    ring_wait(0, 3, 0)

    @pl.loop(0, 2)
    def _(yh):
        update(yh, z // 4)

    for way, q in ((1, 2), (0, 1), (1, 3)):
        ring_wait(way, 3, q)
    for partner in (1, 2):
        relay(0, 3, partner, True).wait_recv()

    @pl.loop(0, 2)
    def _(yh):
        update(yh, 1 - z // 4)

    def member(axis, move):
        if axis == "row":
            dx, dy, dk = move
            return 4 * mod(x + dx, 4) + 2 * mod(y_lo + dy, 2) + mod(core + dk, 2)
        dy, dz = move
        return 8 * mod(y_hi + dy, 2) + mod(z + dz, 8)

    def address(axis, index):
        return (index, col) if axis == "row" else (row, index)

    def rows_of(index):
        return pl.ds(pl.multiple_of(index * ROWS, ROWS), ROWS)

    def gather(stage, axis):
        me = row if axis == "row" else col
        at = gathered.at[stage, rows_of(me)]
        gathered[stage, rows_of(me)] = outgoing[stage]
        for move in MOVES[axis]:
            remote(
                outgoing.at[stage], at, gather_send.at[stage], gather_recv.at[stage], address(axis, member(axis, move))
            ).start()
        every = gathered.at[stage, pl.ds(0, (N - 1) * ROWS)]
        remote(every, every, gather_send.at[stage], gather_recv.at[stage], here).wait()

    centre = jnp.where(row == col, CENTER, 0.0).astype(f32)

    def products(stage):
        if stage % 2 == 0:
            turned_vectors = gathered[stage].T
            blocks = [
                (mod(x + dx, 4), [move for move in MOVES["row"] if move[0] == dx]) for dx in (2, 1, -1, 0)
            ]
        else:
            blocks = [
                (
                    2 * mod(y_hi + dy, 2) + (1 - z // 4 if away else z // 4),
                    [(dy, away, t) for t in ((0, 1, 3, 2) if away else (2, 1, 3, 0)) if dy or away or t],
                )
                for dy in (1, 0) for away in (True, False)
            ]
        for place, moves in blocks:
            span = pl.ds(pl.multiple_of(256 * place, 256), 256)
            if stage % 2 == 0:
                image = jnp.dot(turned_vectors, tile[:, span], preferred_element_type=f32).T
            else:
                image = jnp.dot(tile[span], gathered[stage], preferred_element_type=f32)
            image = image - centre * gathered[stage, span].astype(f32)
            partial[stage, span] = image.astype(bf16)
            whole[span] = image
            for move in moves:
                if stage % 2 == 0:
                    me, to = row, member("row", move)
                    target = (to, col)
                else:
                    me, to = col, 4 * place + mod(lax.rem(z, 4) + move[2], 4)
                    target = (row, to)
                remote(
                    partial.at[stage, rows_of(to)], arrived.at[stage, me], sum_send.at[stage], sum_recv.at[stage], target
                ).start()

    def total_of(stage):
        me = row if stage % 2 == 0 else col
        mine = whole[rows_of(me)]
        every = arrived.at[stage, pl.ds(0, N - 1)]
        remote(every, every, sum_send.at[stage], sum_recv.at[stage], here).wait()
        return mine + jnp.sum(arrived[stage].astype(f32), axis=0)

    def panels_sent():
        for q in (1, 2, 3):
            quad(q).wait_send()

        @pl.when(kind != z)
        def _():
            turn().wait_send()

        for way in (0, 1):
            for step, q in in_flight[way]:
                ring(way, step, q).wait_send()
            for step in range(4 - way):
                for q in (1, 2):
                    relay(way, step, q, False).wait_send()
        piece_sent()

    for stage in range(DEGREES):
        arrived[stage, row if stage % 2 == 0 else col] = jnp.zeros((ROWS, 128), bf16)
        if stage == 0:
            gathered[0] = left[half, :, :, :, ZONE:].reshape(1024, 128)
        else:
            gather(stage, "col" if stage % 2 == 0 else "row")
        products(stage)
        if stage == 0:
            panels_sent()
        total = total_of(stage)
        if stage == 0:
            following = total / HALF_WIDTH
        else:
            following = 2.0 / HALF_WIDTH * total - (start[...] if stage == 1 else history[stage - 2])
        if stage < DEGREES - 1:
            outgoing[stage + 1] = following.astype(bf16)
            history[stage] = following
        else:
            filtered[...] = following


def on_device(tcc_before, shift_panel, source_map, pixels, start_vectors):
    hbm = pl.BlockSpec(memory_space=pltpu.HBM)
    vmem = pl.BlockSpec(memory_space=pltpu.VMEM)
    dma = pltpu.SemaphoreType.DMA
    operands = (tcc_before, shift_panel, source_map.reshape(1, -1), pixels.reshape(1, -1), start_vectors)
    operands = [pltpu.with_memory_space_constraint(operand, pltpu.HBM) for operand in operands]
    return pl.pallas_call(
        body,
        out_shape=(
            jax.ShapeDtypeStruct(start_vectors.shape, f32),
            jax.ShapeDtypeStruct(tcc_before.shape, bf16),
        ),
        in_specs=[hbm] * 5,
        out_specs=(vmem, vmem),
        scratch_shapes=[
            pltpu.VMEM((ROWS, 512), bf16),
            pltpu.VMEM((1, 1024), f32),
            pltpu.VMEM((1, 512), jnp.int32),
            pltpu.VMEM((ROWS, 128), f32),
            pltpu.VMEM((2, 2, 8, ROWS, ZONE + 128), bf16),
            pltpu.VMEM((2, 2, 8, ROWS, ZONE), bf16),
            pltpu.VMEM((DEGREES, 1024, 128), bf16),
            pltpu.VMEM((DEGREES, 1024, 128), bf16),
            pltpu.VMEM((DEGREES, N, ROWS, 128), bf16),
            pltpu.VMEM((DEGREES, ROWS, 128), bf16),
            pltpu.VMEM((1024, 128), f32),
            pltpu.VMEM((DEGREES - 1, ROWS, 128), f32),
            dma((5,)), dma((4,)), dma((4,)), dma((2, 4, 4)), dma((2, 4, 4)), dma((1,)),
            dma((4, 4, 7)), dma((2, 2, 8)), dma((2, 4, 2)), dma((2, 4, 2)),
            dma((DEGREES,)), dma((DEGREES,)), dma((DEGREES,)), dma((DEGREES,)),
        ],
        compiler_params=pltpu.CompilerParams(
            collective_id=0, has_side_effects=True, vmem_limit_bytes=32 * 1024 * 1024
        ),
    )(*operands)


def solution(mesh):
    in_specs = (P("row", "col"), P(("row", "col"), None), P(), P(), P(("row", "col"), None))
    out_specs = (P(("row", "col"), None), P("row", "col"))
    return jax.shard_map(
        on_device, mesh=mesh, in_specs=in_specs, out_specs=out_specs, check_vma=False
    )
```

```python
import jax
import jax.numpy as jnp
from jax import lax
from jax.experimental import pallas as pl
from jax.experimental.pallas import tpu as pltpu
from jax.sharding import PartitionSpec as P

DEGREES = 4
CENTER = 0.45
HALF_WIDTH = 1.6
MESH = pl.DeviceIdType.MESH
N = 16
ROWS = 64
ZONE = 512
WINDOW = 4


def farthest_first(moves, hops):
    return sorted(moves, key=lambda move: -hops(*move))


MOVES = {
    "row": farthest_first(
        [(dx, dy, dk) for dx in (2, 1, -1, 0) for dy in (1, 0) for dk in (1, 0) if dx or dy or dk],
        lambda dx, dy, dk: abs(dx) + dy,
    ),
    "col": farthest_first(
        [(dy, dz) for dy in (1, 0) for dz in (4, 3, -3, 2, -2, 1, -1, 0) if dy or dz],
        lambda dy, dz: 2 * dy + abs(dz),
    ),
}
f32 = jnp.float32
bf16 = jnp.bfloat16


def mod(value, size):
    return lax.rem(value + size, size)


def device(x, y, core, z):
    x, y, z = mod(x, 4), mod(y, 4), mod(z, 8)
    return (4 * x + 2 * lax.rem(y, 2) + core, 8 * (y // 2) + z)


def body(
    before, panel_in, source_in, pixels_in, start_in, filtered, tile,
    panel, source, pixels, start, left, right, gathered, partial, arrived, outgoing,
    whole, history,
    tcc_sem, quad_send, quad_recv, ring_send, ring_recv, turn_send,
    piece_send, piece_recv, relay_send, relay_recv, gather_send, gather_recv, sum_send, sum_recv,
):
    row, col = lax.axis_index("row"), lax.axis_index("col")
    x, y_lo, core = row // 4, lax.rem(row // 2, 2), lax.rem(row, 2)
    y_hi, z = col // 8, lax.rem(col, 8)
    y = 2 * y_hi + y_lo
    half = x // 2
    kind = lax.rem(row, 8)
    here = (row, col)
    sibling = (row + 1 - 2 * core, col)

    loads = [
        pltpu.make_async_copy(src, dst, tcc_sem.at[1 + i])
        for i, (src, dst) in enumerate(
            ((pixels_in, pixels), (source_in, source), (panel_in, panel), (start_in, start))
        )
    ]
    for small in loads:
        small.start()
    load = pltpu.make_async_copy(before, tile, tcc_sem.at[0])
    load.start()

    barrier = pltpu.get_barrier_semaphore()

    @pl.loop(1, N)
    def _(step):
        pl.semaphore_signal(barrier, 1, device_id=(mod(row + step, N), col), device_id_type=MESH)
        pl.semaphore_signal(barrier, 1, device_id=(row, mod(col + step, N)), device_id_type=MESH)

    far = jnp.where(y_lo == 0, y - 1, y + 1)
    swapped = (8 * half + z, 8 * y_hi + kind)
    for to in (device(x, far + 4, core, z), device(x + 2, y + 2, core, z), swapped):
        pl.semaphore_signal(barrier, 1, device_id=to, device_id_type=MESH)

    for small in loads:
        small.wait()
    src = jnp.broadcast_to(source[...], (N, source.shape[1]))
    high = src.astype(bf16).astype(f32)
    middle = (src - high).astype(bf16).astype(f32)
    low = src - high - middle
    part = lax.broadcasted_iota(jnp.int32, src.shape, 0)
    parts = jnp.where(part == 0, high, jnp.where(part == 1, middle, jnp.where(part == 2, low, 0.0)))
    place = lax.broadcasted_iota(jnp.int32, (source.shape[1], pixels.shape[1]), 0)
    hit = jnp.where(place == pixels[...], 1.0, 0.0).astype(bf16)
    three = jnp.dot(parts.astype(bf16), hit, preferred_element_type=f32)
    weight = three[0:1] + three[1:2] + three[2:3]
    scaled = (panel[...].astype(f32) * jnp.sqrt(weight)).astype(bf16)
    left[half, y_hi, z, :, :ZONE] = scaled
    left[half, y_hi, z, :, ZONE:] = start[...].astype(bf16)

    @pl.when(kind == z)
    def _():
        right[half, y_hi, z] = scaled

    pl.semaphore_wait(barrier, 2 * (N - 1) + 3)

    def remote(src_ref, dst_ref, send, recv, to):
        return pltpu.make_async_remote_copy(
            src_ref=src_ref, dst_ref=dst_ref, send_sem=send, recv_sem=recv, device_id=to, device_id_type=MESH
        )

    def turn():
        return remote(
            left.at[half, y_hi, z, :, pl.ds(0, ZONE)], right.at[half, y_hi, z], turn_send.at[0],
            piece_recv.at[half, y_hi, z], swapped,
        )

    @pl.when(kind != z)
    def _():
        turn().start()

    def chip(i, j):
        along_x, along_y = jnp.where(core == 0, i, j), jnp.where(core == 0, j, i)
        return mod(x + along_x, 4), mod(y + along_y, 4)

    def place_of(cx, cy, k):
        return cx // 2, cy // 2, 4 * lax.rem(cx, 2) + 2 * lax.rem(cy, 2) + k

    def piece_copy(i, j, way):
        at = place_of(*chip(i, j), core)
        if way is None:
            index, to = 6, sibling
        else:
            tx, ty = chip(*way)
            index, to = (way[0] or 3 + way[1]) - 1, device(tx, ty, core, z)
        return remote(right.at[at], right.at[at], piece_send.at[i, j, index], piece_recv.at[at], to)

    def piece_wait(i, j, k=None):
        cx, cy = chip(i, j)
        at = place_of(cx, cy, core if k is None else k)
        remote(right.at[at], right.at[at], turn_send.at[0], piece_recv.at[at], here).wait_recv()

    def piece_first():
        @pl.when(kind != z)
        def _():
            piece_wait(0, 0)

        for d in (2, 1, 3):
            piece_copy(0, 0, (d, 0)).start()
        for d in (2, 1, 3):
            piece_copy(0, 0, (0, d)).start()
        piece_copy(0, 0, None).start()

    def piece_second():
        for i in (1, 3, 2):
            piece_wait(i, 0)
            for d in (2, 1, 3):
                piece_copy(i, 0, (0, d)).start()
            piece_copy(i, 0, None).start()

    def piece_third():
        for i in (0, 1, 3, 2):
            for j in (1, 3, 2):
                piece_wait(i, j)
                piece_copy(i, j, None).start()

    def piece_last():
        for i in range(4):
            for j in range(4):
                piece_wait(i, j, 1 - core)

    def piece_sent():
        for i in range(4):
            for j in range(4):
                piece_copy(i, j, None).wait_send()
                if j == 0:
                    for d in (1, 2, 3):
                        piece_copy(i, 0, (0, d)).wait_send()
                        if i == 0:
                            piece_copy(0, 0, (d, 0)).wait_send()

    def piece_of(q, zz):
        h, yh = mod(half + q % 2, 2), mod(y_hi + q // 2, 2)
        return left.at[h, yh, zz] if q % 2 == 0 else left.at[h, yh, zz, :, pl.ds(0, ZONE)]

    def quad(q):
        own = left.at[half, y_hi, z]
        own = own if q % 2 == 0 else left.at[half, y_hi, z, :, pl.ds(0, ZONE)]
        return remote(own, own, quad_send.at[q], quad_recv.at[q], device(x + 2 * (q % 2), y + 2 * (q // 2), core, z))

    def quad_wait(q):
        there = piece_of(q, z)
        remote(there, there, quad_send.at[q], quad_recv.at[q], here).wait_recv()

    def travelling(q, zz):
        if q == 1:
            return left.at[1 - half, y_hi, zz, pl.ds(0, 32), pl.ds(0, ZONE)]
        if q == 2:
            return left.at[half, 1 - y_hi, zz, pl.ds(0, 32)]
        return piece_of(q, zz)

    def relay(way, step, q, arriving):
        h, yh = (half, y_hi) if not arriving else (1 - half, y_hi) if q == 1 else (half, 1 - y_hi)
        zz, upper = mod(z - step - 1 if way == 0 else z + step + 1, 8), pl.ds(32, 32)
        at = left.at[h, yh, zz, upper, pl.ds(0, ZONE)] if q == 1 else left.at[h, yh, zz, upper]
        to = here if arriving else device(x + 2 * (q % 2), y + 2 * (q // 2), core, z)
        return remote(at, at, relay_send.at[way, step, q - 1], relay_recv.at[way, step, q - 1], to)

    def ring(way, step, q):
        at = travelling(q, mod(z - step if way == 0 else z + step, 8))
        return remote(
            at, at, ring_send.at[way, step, q], ring_recv.at[way, step, q],
            device(x, y, core, z + 1 if way == 0 else z + 7),
        )

    def ring_wait(way, step, q):
        at = travelling(q, mod(z - step - 1 if way == 0 else z + step + 1, 8))
        remote(at, at, ring_send.at[way, step, q], ring_recv.at[way, step, q], here).wait_recv()
        if q == 0:
            for partner in (1, 2):
                relay(way, step, partner, False).start()

    in_flight = [[], []]

    def ring_start(way, step, q):
        if len(in_flight[way]) == WINDOW:
            ring(way, *in_flight[way].pop(0)).wait_send()
        ring(way, step, q).start()
        in_flight[way].append((step, q))

    def ring_go(step, q):
        if step == 0 and q > 0:
            quad_wait(q)
        for way in (0, 1):
            if step > 0:
                ring_wait(way, step - 1, q)
            if step < 3 or (q < 2) == (way == 0):
                ring_start(way, step, q)

    for q in (3, 1, 2):
        quad(q).start()
    for q in range(4):
        ring_go(0, q)
    piece_first()
    for q in range(4):
        ring_go(1, q)
    piece_second()
    for q in range(4):
        ring_go(2, q)
    for q in range(4):
        ring_go(3, q)
    piece_third()
    piece_last()
    load.wait()
    for step in range(3):
        for way in (0, 1):
            for partner in (1, 2):
                relay(way, step, partner, True).wait_recv()

    sign = jnp.where(half == y_hi, 1.0, -1.0).astype(f32)
    nt = (((1,), (1,)), ((), ()))

    def update(yh, quarter):
        zs = pl.ds(4 * quarter, 4)
        span = pl.ds(pl.multiple_of(512 * yh + 256 * quarter, 256), 256)
        straight = lax.dot_general(
            left[half, yh, zs, :, :ZONE].reshape(256, ZONE), right[y_hi].reshape(1024, ZONE), nt,
            preferred_element_type=f32,
        )
        turned = lax.dot_general(
            left[1 - half, yh, zs, :, :ZONE].reshape(256, ZONE), right[1 - y_hi].reshape(1024, ZONE), nt,
            preferred_element_type=f32,
        )
        tile[span] = (tile[span].astype(f32) + (straight + sign * turned)).astype(bf16)

    ring_wait(0, 3, 0)

    @pl.loop(0, 4)
    def _(i):
        @pl.when(i == 2)
        def _():
            for way, q in ((1, 2), (0, 1), (1, 3)):
                ring_wait(way, 3, q)
            for partner in (1, 2):
                relay(0, 3, partner, True).wait_recv()

        update(lax.rem(i, 2), lax.rem(z // 4 + i // 2, 2))

    def member(axis, move):
        if axis == "row":
            dx, dy, dk = move
            return 4 * mod(x + dx, 4) + 2 * mod(y_lo + dy, 2) + mod(core + dk, 2)
        dy, dz = move
        return 8 * mod(y_hi + dy, 2) + mod(z + dz, 8)

    def address(axis, index):
        return (index, col) if axis == "row" else (row, index)

    def rows_of(index):
        return pl.ds(pl.multiple_of(index * ROWS, ROWS), ROWS)

    def gather(stage, axis):
        me = row if axis == "row" else col
        at = gathered.at[stage, rows_of(me)]
        for move in MOVES[axis]:
            remote(
                outgoing.at[stage], at, gather_send.at[stage], gather_recv.at[stage], address(axis, member(axis, move))
            ).start()
        gathered[stage, rows_of(me)] = outgoing[stage]
        every = gathered.at[stage, pl.ds(0, (N - 1) * ROWS)]
        remote(every, every, gather_send.at[stage], gather_recv.at[stage], here).wait()

    centre = jnp.where(row == col, CENTER, 0.0).astype(f32)

    def products(stage):
        if stage % 2 == 0:
            turned_vectors = gathered[stage].T
            blocks = [
                (mod(x + dx, 4), [move for move in MOVES["row"] if move[0] == dx]) for dx in (2, 1, -1, 0)
            ]
        else:
            blocks = [
                (
                    2 * mod(y_hi + dy, 2) + (1 - z // 4 if away else z // 4),
                    [(dy, away, t) for t in ((0, 1, 3, 2) if away else (2, 1, 3, 0)) if dy or away or t],
                )
                for dy in (1, 0) for away in (True, False)
            ]
        for place, moves in blocks:
            span = pl.ds(pl.multiple_of(256 * place, 256), 256)
            if stage % 2 == 0:
                image = jnp.dot(turned_vectors, tile[:, span], preferred_element_type=f32).T
            else:
                image = jnp.dot(tile[span], gathered[stage], preferred_element_type=f32)
            image = image - centre * gathered[stage, span].astype(f32)
            partial[stage, span] = image.astype(bf16)
            whole[span] = image
            for move in moves:
                if stage % 2 == 0:
                    me, to = row, member("row", move)
                    target = (to, col)
                else:
                    me, to = col, 4 * place + mod(lax.rem(z, 4) + move[2], 4)
                    target = (row, to)
                remote(
                    partial.at[stage, rows_of(to)], arrived.at[stage, me], sum_send.at[stage], sum_recv.at[stage], target
                ).start()

    def total_of(stage):
        me = row if stage % 2 == 0 else col
        mine = whole[rows_of(me)]
        every = arrived.at[stage, pl.ds(0, N - 1)]
        remote(every, every, sum_send.at[stage], sum_recv.at[stage], here).wait()
        return mine + jnp.sum(arrived[stage].astype(f32), axis=0)

    def panels_sent():
        for q in (1, 2, 3):
            quad(q).wait_send()

        @pl.when(kind != z)
        def _():
            turn().wait_send()

        for way in (0, 1):
            for step, q in in_flight[way]:
                ring(way, step, q).wait_send()
            for step in range(4 - way):
                for q in (1, 2):
                    relay(way, step, q, False).wait_send()
        piece_sent()

    for stage in range(DEGREES):
        arrived[stage, row if stage % 2 == 0 else col] = jnp.zeros((ROWS, 128), bf16)
        if stage == 0:
            gathered[0] = left[half, :, :, :, ZONE:].reshape(1024, 128)
        else:
            gather(stage, "col" if stage % 2 == 0 else "row")
        products(stage)
        if stage == 0:
            panels_sent()
        total = total_of(stage)
        if stage == 0:
            following = total / HALF_WIDTH
        else:
            following = 2.0 / HALF_WIDTH * total - (start[...] if stage == 1 else history[stage - 2])
        if stage < DEGREES - 1:
            outgoing[stage + 1] = following.astype(bf16)
            history[stage] = following
        else:
            filtered[...] = following


def on_device(tcc_before, shift_panel, source_map, pixels, start_vectors):
    hbm = pl.BlockSpec(memory_space=pltpu.HBM)
    vmem = pl.BlockSpec(memory_space=pltpu.VMEM)
    dma = pltpu.SemaphoreType.DMA
    operands = (tcc_before, shift_panel, source_map.reshape(1, -1), pixels.reshape(1, -1), start_vectors)
    operands = [pltpu.with_memory_space_constraint(operand, pltpu.HBM) for operand in operands]
    return pl.pallas_call(
        body,
        out_shape=(
            jax.ShapeDtypeStruct(start_vectors.shape, f32),
            jax.ShapeDtypeStruct(tcc_before.shape, bf16),
        ),
        in_specs=[hbm] * 5,
        out_specs=(vmem, vmem),
        scratch_shapes=[
            pltpu.VMEM((ROWS, 512), bf16),
            pltpu.VMEM((1, 1024), f32),
            pltpu.VMEM((1, 512), jnp.int32),
            pltpu.VMEM((ROWS, 128), f32),
            pltpu.VMEM((2, 2, 8, ROWS, ZONE + 128), bf16),
            pltpu.VMEM((2, 2, 8, ROWS, ZONE), bf16),
            pltpu.VMEM((DEGREES, 1024, 128), bf16),
            pltpu.VMEM((DEGREES, 1024, 128), bf16),
            pltpu.VMEM((DEGREES, N, ROWS, 128), bf16),
            pltpu.VMEM((DEGREES, ROWS, 128), bf16),
            pltpu.VMEM((1024, 128), f32),
            pltpu.VMEM((DEGREES - 1, ROWS, 128), f32),
            dma((5,)), dma((4,)), dma((4,)), dma((2, 4, 4)), dma((2, 4, 4)), dma((1,)),
            dma((4, 4, 7)), dma((2, 2, 8)), dma((2, 4, 2)), dma((2, 4, 2)),
            dma((DEGREES,)), dma((DEGREES,)), dma((DEGREES,)), dma((DEGREES,)),
        ],
        compiler_params=pltpu.CompilerParams(
            collective_id=0, has_side_effects=True, vmem_limit_bytes=32 * 1024 * 1024
        ),
    )(*operands)


def solution(mesh):
    in_specs = (P("row", "col"), P(("row", "col"), None), P(), P(), P(("row", "col"), None))
    out_specs = (P(("row", "col"), None), P("row", "col"))
    return jax.shard_map(
        on_device, mesh=mesh, in_specs=in_specs, out_specs=out_specs, check_vma=False
    )
```

```python
import jax
import jax.numpy as jnp
from jax import lax
from jax.experimental import pallas as pl
from jax.experimental.pallas import tpu as pltpu
from jax.sharding import PartitionSpec as P

DEGREES = 4
CENTER = 0.45
HALF_WIDTH = 1.6
MESH = pl.DeviceIdType.MESH
N = 16
ROWS = 64
ZONE = 512
WINDOW = 4


def farthest_first(moves, hops):
    return sorted(moves, key=lambda move: -hops(*move))


MOVES = {
    "row": farthest_first(
        [(dx, dy, dk) for dx in (2, 1, -1, 0) for dy in (1, 0) for dk in (1, 0) if dx or dy or dk],
        lambda dx, dy, dk: abs(dx) + dy,
    ),
    "col": farthest_first(
        [(dy, dz) for dy in (1, 0) for dz in (4, 3, -3, 2, -2, 1, -1, 0) if dy or dz],
        lambda dy, dz: 2 * dy + abs(dz),
    ),
}
f32 = jnp.float32
bf16 = jnp.bfloat16


def mod(value, size):
    return lax.rem(value + size, size)


def device(x, y, core, z):
    x, y, z = mod(x, 4), mod(y, 4), mod(z, 8)
    return (4 * x + 2 * lax.rem(y, 2) + core, 8 * (y // 2) + z)


def body(
    before, panel_in, source_in, pixels_in, start_in, filtered, tile,
    panel, source, pixels, start, left, right, gathered, partial, arrived, outgoing,
    whole, history,
    tcc_sem, quad_send, quad_recv, ring_send, ring_recv, turn_send,
    piece_send, piece_recv, relay_send, relay_recv, gather_send, gather_recv, sum_send, sum_recv,
):
    row, col = lax.axis_index("row"), lax.axis_index("col")
    x, y_lo, core = row // 4, lax.rem(row // 2, 2), lax.rem(row, 2)
    y_hi, z = col // 8, lax.rem(col, 8)
    y = 2 * y_hi + y_lo
    half = x // 2
    kind = lax.rem(row, 8)
    here = (row, col)
    sibling = (row + 1 - 2 * core, col)

    loads = [
        pltpu.make_async_copy(src, dst, tcc_sem.at[1 + i])
        for i, (src, dst) in enumerate(
            ((pixels_in, pixels), (source_in, source), (panel_in, panel), (start_in, start))
        )
    ]
    for small in loads:
        small.start()
    load = pltpu.make_async_copy(before, tile, tcc_sem.at[0])
    load.start()

    barrier = pltpu.get_barrier_semaphore()

    @pl.loop(1, N)
    def _(step):
        pl.semaphore_signal(barrier, 1, device_id=(mod(row + step, N), col), device_id_type=MESH)
        pl.semaphore_signal(barrier, 1, device_id=(row, mod(col + step, N)), device_id_type=MESH)

    far = jnp.where(y_lo == 0, y - 1, y + 1)
    swapped = (8 * half + z, 8 * y_hi + kind)
    for to in (device(x, far + 4, core, z), device(x + 2, y + 2, core, z), swapped):
        pl.semaphore_signal(barrier, 1, device_id=to, device_id_type=MESH)

    for small in loads:
        small.wait()
    src = jnp.broadcast_to(source[...], (N, source.shape[1]))
    high = src.astype(bf16).astype(f32)
    middle = (src - high).astype(bf16).astype(f32)
    low = src - high - middle
    part = lax.broadcasted_iota(jnp.int32, src.shape, 0)
    parts = jnp.where(part == 0, high, jnp.where(part == 1, middle, jnp.where(part == 2, low, 0.0)))
    place = lax.broadcasted_iota(jnp.int32, (source.shape[1], pixels.shape[1]), 0)
    hit = jnp.where(place == pixels[...], 1.0, 0.0).astype(bf16)
    three = jnp.dot(parts.astype(bf16), hit, preferred_element_type=f32)
    weight = three[0:1] + three[1:2] + three[2:3]
    scaled = (panel[...].astype(f32) * jnp.sqrt(weight)).astype(bf16)
    left[half, y_hi, z, :, :ZONE] = scaled
    left[half, y_hi, z, :, ZONE:] = start[...].astype(bf16)

    @pl.when(kind == z)
    def _():
        right[half, y_hi, z] = scaled

    pl.semaphore_wait(barrier, 2 * (N - 1) + 3)

    def remote(src_ref, dst_ref, send, recv, to):
        return pltpu.make_async_remote_copy(
            src_ref=src_ref, dst_ref=dst_ref, send_sem=send, recv_sem=recv, device_id=to, device_id_type=MESH
        )

    def turn():
        return remote(
            left.at[half, y_hi, z, :, pl.ds(0, ZONE)], right.at[half, y_hi, z], turn_send.at[0],
            piece_recv.at[half, y_hi, z], swapped,
        )

    @pl.when(kind != z)
    def _():
        turn().start()

    def chip(i, j):
        along_x, along_y = jnp.where(core == 0, i, j), jnp.where(core == 0, j, i)
        return mod(x + along_x, 4), mod(y + along_y, 4)

    def place_of(cx, cy, k):
        return cx // 2, cy // 2, 4 * lax.rem(cx, 2) + 2 * lax.rem(cy, 2) + k

    def piece_copy(i, j, way):
        at = place_of(*chip(i, j), core)
        if way is None:
            index, to = 6, sibling
        else:
            tx, ty = chip(*way)
            index, to = (way[0] or 3 + way[1]) - 1, device(tx, ty, core, z)
        return remote(right.at[at], right.at[at], piece_send.at[i, j, index], piece_recv.at[at], to)

    def piece_wait(i, j, k=None):
        cx, cy = chip(i, j)
        at = place_of(cx, cy, core if k is None else k)
        remote(right.at[at], right.at[at], turn_send.at[0], piece_recv.at[at], here).wait_recv()

    def piece_first():
        @pl.when(kind != z)
        def _():
            piece_wait(0, 0)

        for d in (2, 1, 3):
            piece_copy(0, 0, (d, 0)).start()
        for d in (2, 1, 3):
            piece_copy(0, 0, (0, d)).start()
        piece_copy(0, 0, None).start()

    def piece_second():
        for i in (1, 3, 2):
            piece_wait(i, 0)
            for d in (2, 1, 3):
                piece_copy(i, 0, (0, d)).start()
            piece_copy(i, 0, None).start()

    def piece_third(which):
        for i in which:
            for j in (1, 3, 2):
                piece_wait(i, j)
                piece_copy(i, j, None).start()

    def piece_last():
        for i in range(4):
            for j in range(4):
                piece_wait(i, j, 1 - core)

    def piece_sent():
        for i in range(4):
            for j in range(4):
                piece_copy(i, j, None).wait_send()
                if j == 0:
                    for d in (1, 2, 3):
                        piece_copy(i, 0, (0, d)).wait_send()
                        if i == 0:
                            piece_copy(0, 0, (d, 0)).wait_send()

    def piece_of(q, zz):
        h, yh = mod(half + q % 2, 2), mod(y_hi + q // 2, 2)
        return left.at[h, yh, zz] if q % 2 == 0 else left.at[h, yh, zz, :, pl.ds(0, ZONE)]

    def quad(q):
        own = left.at[half, y_hi, z]
        own = own if q % 2 == 0 else left.at[half, y_hi, z, :, pl.ds(0, ZONE)]
        return remote(own, own, quad_send.at[q], quad_recv.at[q], device(x + 2 * (q % 2), y + 2 * (q // 2), core, z))

    def quad_wait(q):
        there = piece_of(q, z)
        remote(there, there, quad_send.at[q], quad_recv.at[q], here).wait_recv()

    def travelling(q, zz):
        if q == 1:
            return left.at[1 - half, y_hi, zz, pl.ds(0, 32), pl.ds(0, ZONE)]
        if q == 2:
            return left.at[half, 1 - y_hi, zz, pl.ds(0, 32)]
        return piece_of(q, zz)

    def relay(way, step, q, arriving):
        h, yh = (half, y_hi) if not arriving else (1 - half, y_hi) if q == 1 else (half, 1 - y_hi)
        zz, upper = mod(z - step - 1 if way == 0 else z + step + 1, 8), pl.ds(32, 32)
        at = left.at[h, yh, zz, upper, pl.ds(0, ZONE)] if q == 1 else left.at[h, yh, zz, upper]
        to = here if arriving else device(x + 2 * (q % 2), y + 2 * (q // 2), core, z)
        return remote(at, at, relay_send.at[way, step, q - 1], relay_recv.at[way, step, q - 1], to)

    def ring(way, step, q):
        at = travelling(q, mod(z - step if way == 0 else z + step, 8))
        return remote(
            at, at, ring_send.at[way, step, q], ring_recv.at[way, step, q],
            device(x, y, core, z + 1 if way == 0 else z + 7),
        )

    def ring_wait(way, step, q):
        at = travelling(q, mod(z - step - 1 if way == 0 else z + step + 1, 8))
        remote(at, at, ring_send.at[way, step, q], ring_recv.at[way, step, q], here).wait_recv()
        if q == 0:
            for partner in (1, 2):
                relay(way, step, partner, False).start()

    in_flight = [[], []]

    def ring_start(way, step, q):
        if len(in_flight[way]) == WINDOW:
            ring(way, *in_flight[way].pop(0)).wait_send()
        ring(way, step, q).start()
        in_flight[way].append((step, q))

    def ring_go(step, q):
        if step == 0 and q > 0:
            quad_wait(q)
        for way in (0, 1):
            if step > 0:
                ring_wait(way, step - 1, q)
            if step < 3 or (q < 2) == (way == 0):
                ring_start(way, step, q)

    for q in (3, 1, 2):
        quad(q).start()
    for q in (0, 1, 2, 3):
        ring_go(0, q)
    piece_first()
    for q in (0, 1, 2, 3):
        ring_go(1, q)
    piece_second()
    for q in (0, 1, 2, 3):
        ring_go(2, q)
    piece_third((0,))
    for q in (0, 1, 2, 3):
        ring_go(3, q)
    piece_third((1, 3, 2))
    piece_last()
    load.wait()
    for step in range(3):
        for way in (0, 1):
            for partner in (1, 2):
                relay(way, step, partner, True).wait_recv()

    sign = jnp.where(half == y_hi, 1.0, -1.0).astype(f32)
    nt = (((1,), (1,)), ((), ()))

    def update(yh, quarter):
        zs = pl.ds(4 * quarter, 4)
        span = pl.ds(pl.multiple_of(512 * yh + 256 * quarter, 256), 256)
        straight = lax.dot_general(
            left[half, yh, zs, :, :ZONE].reshape(256, ZONE), right[y_hi].reshape(1024, ZONE), nt,
            preferred_element_type=f32,
        )
        turned = lax.dot_general(
            left[1 - half, yh, zs, :, :ZONE].reshape(256, ZONE), right[1 - y_hi].reshape(1024, ZONE), nt,
            preferred_element_type=f32,
        )
        tile[span] = (tile[span].astype(f32) + (straight + sign * turned)).astype(bf16)

    ring_wait(0, 3, 0)

    @pl.loop(0, 4)
    def _(i):
        @pl.when(i == 2)
        def _():
            for way, q in ((1, 2), (0, 1), (1, 3)):
                ring_wait(way, 3, q)
            for partner in (1, 2):
                relay(0, 3, partner, True).wait_recv()

        update(lax.rem(i, 2), lax.rem(z // 4 + i // 2, 2))

    def member(axis, move):
        if axis == "row":
            dx, dy, dk = move
            return 4 * mod(x + dx, 4) + 2 * mod(y_lo + dy, 2) + mod(core + dk, 2)
        dy, dz = move
        return 8 * mod(y_hi + dy, 2) + mod(z + dz, 8)

    def address(axis, index):
        return (index, col) if axis == "row" else (row, index)

    def rows_of(index):
        return pl.ds(pl.multiple_of(index * ROWS, ROWS), ROWS)

    def gather(stage, axis):
        me = row if axis == "row" else col
        at = gathered.at[stage, rows_of(me)]
        for move in MOVES[axis]:
            remote(
                outgoing.at[stage], at, gather_send.at[stage], gather_recv.at[stage], address(axis, member(axis, move))
            ).start()
        gathered[stage, rows_of(me)] = outgoing[stage]
        every = gathered.at[stage, pl.ds(0, (N - 1) * ROWS)]
        remote(every, every, gather_send.at[stage], gather_recv.at[stage], here).wait()

    centre = jnp.where(row == col, CENTER, 0.0).astype(f32)

    def products(stage):
        if stage % 2 == 0:
            turned_vectors = gathered[stage].T
            blocks = [
                (mod(x + dx, 4), [move for move in MOVES["row"] if move[0] == dx]) for dx in (2, 1, -1, 0)
            ]
        else:
            blocks = [
                (
                    2 * mod(y_hi + dy, 2) + (1 - z // 4 if away else z // 4),
                    [(dy, away, t) for t in ((0, 1, 3, 2) if away else (2, 1, 3, 0)) if dy or away or t],
                )
                for dy in (1, 0) for away in (True, False)
            ]
        for place, moves in blocks:
            span = pl.ds(pl.multiple_of(256 * place, 256), 256)
            if stage % 2 == 0:
                image = jnp.dot(turned_vectors, tile[:, span], preferred_element_type=f32).T
            else:
                image = jnp.dot(tile[span], gathered[stage], preferred_element_type=f32)
            image = image - centre * gathered[stage, span].astype(f32)
            partial[stage, span] = image.astype(bf16)
            whole[span] = image
            for move in moves:
                if stage % 2 == 0:
                    me, to = row, member("row", move)
                    target = (to, col)
                else:
                    me, to = col, 4 * place + mod(lax.rem(z, 4) + move[2], 4)
                    target = (row, to)
                remote(
                    partial.at[stage, rows_of(to)], arrived.at[stage, me], sum_send.at[stage], sum_recv.at[stage], target
                ).start()

    def total_of(stage):
        me = row if stage % 2 == 0 else col
        mine = whole[rows_of(me)]
        every = arrived.at[stage, pl.ds(0, N - 1)]
        remote(every, every, sum_send.at[stage], sum_recv.at[stage], here).wait()
        return mine + jnp.sum(arrived[stage].astype(f32), axis=0)

    def panels_sent():
        for q in (1, 2, 3):
            quad(q).wait_send()

        @pl.when(kind != z)
        def _():
            turn().wait_send()

        for way in (0, 1):
            for step, q in in_flight[way]:
                ring(way, step, q).wait_send()
            for step in range(4 - way):
                for q in (1, 2):
                    relay(way, step, q, False).wait_send()
        piece_sent()

    for stage in range(DEGREES):
        arrived[stage, row if stage % 2 == 0 else col] = jnp.zeros((ROWS, 128), bf16)
        if stage == 0:
            gathered[0] = left[half, :, :, :, ZONE:].reshape(1024, 128)
        else:
            gather(stage, "col" if stage % 2 == 0 else "row")
        products(stage)
        if stage == 0:
            panels_sent()
        total = total_of(stage)
        if stage == 0:
            following = total / HALF_WIDTH
        else:
            following = 2.0 / HALF_WIDTH * total - (start[...] if stage == 1 else history[stage - 2])
        if stage < DEGREES - 1:
            outgoing[stage + 1] = following.astype(bf16)
            history[stage] = following
        else:
            filtered[...] = following


def on_device(tcc_before, shift_panel, source_map, pixels, start_vectors):
    hbm = pl.BlockSpec(memory_space=pltpu.HBM)
    vmem = pl.BlockSpec(memory_space=pltpu.VMEM)
    dma = pltpu.SemaphoreType.DMA
    operands = (tcc_before, shift_panel, source_map.reshape(1, -1), pixels.reshape(1, -1), start_vectors)
    operands = [pltpu.with_memory_space_constraint(operand, pltpu.HBM) for operand in operands]
    return pl.pallas_call(
        body,
        out_shape=(
            jax.ShapeDtypeStruct(start_vectors.shape, f32),
            jax.ShapeDtypeStruct(tcc_before.shape, bf16),
        ),
        in_specs=[hbm] * 5,
        out_specs=(vmem, vmem),
        scratch_shapes=[
            pltpu.VMEM((ROWS, 512), bf16),
            pltpu.VMEM((1, 1024), f32),
            pltpu.VMEM((1, 512), jnp.int32),
            pltpu.VMEM((ROWS, 128), f32),
            pltpu.VMEM((2, 2, 8, ROWS, ZONE + 128), bf16),
            pltpu.VMEM((2, 2, 8, ROWS, ZONE), bf16),
            pltpu.VMEM((DEGREES, 1024, 128), bf16),
            pltpu.VMEM((DEGREES, 1024, 128), bf16),
            pltpu.VMEM((DEGREES, N, ROWS, 128), bf16),
            pltpu.VMEM((DEGREES, ROWS, 128), bf16),
            pltpu.VMEM((1024, 128), f32),
            pltpu.VMEM((DEGREES - 1, ROWS, 128), f32),
            dma((5,)), dma((4,)), dma((4,)), dma((2, 4, 4)), dma((2, 4, 4)), dma((1,)),
            dma((4, 4, 7)), dma((2, 2, 8)), dma((2, 4, 2)), dma((2, 4, 2)),
            dma((DEGREES,)), dma((DEGREES,)), dma((DEGREES,)), dma((DEGREES,)),
        ],
        compiler_params=pltpu.CompilerParams(
            collective_id=0, has_side_effects=True, vmem_limit_bytes=32 * 1024 * 1024
        ),
    )(*operands)


def solution(mesh):
    in_specs = (P("row", "col"), P(("row", "col"), None), P(), P(), P(("row", "col"), None))
    out_specs = (P(("row", "col"), None), P("row", "col"))
    return jax.shard_map(
        on_device, mesh=mesh, in_specs=in_specs, out_specs=out_specs, check_vma=False
    )
```
